256 devices in a mesh: slab: 32 (over x, z), col: 4 (over y), pb: 2 (over core).
Axes of the slice: x: 4, y: 4, z: 8, core: 2. Of those that a mesh axis runs over, the one named last changes fastest.
Arguments:
- queries_raw: float32 [1024, 768], P(('slab', 'col', 'pb')), may hold values from -1.5 to 1.5
- projection: float32 [768, 768], replicated, may hold values from -0.21875 to 0.21875
- passages: bfloat16 [524288, 768], P(('slab', 'col')), may hold values from -17 to 17
- positives: int32 [1024, 4], P(('slab', 'col', 'pb')), may hold values from 0 to 524287
Outputs:
- loss: float32 [1024], P(('slab', 'col', 'pb'))
- grad_raw: float32 [1024, 768], P(('slab', 'col', 'pb'))
- grad_projection: float32 [768, 768], replicated
The draws below stay inside these ranges and needn't reach their ends.
All inputs are finite; a program needn't handle non-finite values.
Results may differ from the reference program's by a relative error of at most 0.0053.
Values may be sent and summed in bfloat16 or wider, within the bound.
No kernel may reach another device: no remote copies, remote signals or barrier semaphores. Data moves between devices by JAX's collectives and lax.ppermute only.
A program may use at most 128 MiB of HBM per device.

```python
import math
import jax
import jax.numpy as jnp
import numpy as np
from jax import lax

D = 768
POS = 4
NP = 524288
Q = 1024


def draw_passages(key, part):
    key_perm, key_centres, key_mask, key_dims, key_rows, key_jitter = jax.random.split(jax.random.fold_in(key, 7), 6)
    cluster_count = max(NP // 128, 8)
    row_ids = jnp.arange(NP, dtype=jnp.int32)
    groups = jax.random.permutation(key_perm, NP) % cluster_count
    row_ramp = 1.0 + 2.0 * row_ids.astype(jnp.float32)[:, None] / NP
    keep = jax.random.uniform(key_mask, (cluster_count, D), jnp.float32) < 0.25
    dim_spread = jnp.exp(jax.random.uniform(key_dims, (cluster_count, D), jnp.float32, math.log(0.08), math.log(0.6)))
    centres = jnp.clip(1.2 * jax.random.normal(key_centres, (cluster_count, D), jnp.float32), -2.5, 2.5)
    row_scale = jnp.exp(jax.random.uniform(key_rows, (NP, 1), jnp.float32, math.log(0.3), math.log(1.5)))
    jitter = jnp.clip(jax.random.normal(key_jitter, (NP, D), jnp.float32), -2.0, 2.0)
    centres = jnp.where(keep, centres, 0.0)
    values_out = (centres[groups] + jitter * dim_spread[groups]) * row_scale * row_ramp
    return values_out.astype(jnp.bfloat16)


def set_ends(values, own_key, smallest, largest):
    dims = values.shape
    spot = [jax.random.randint(jax.random.fold_in(own_key, axis), (), 0, dims[axis]) for axis in range(len(dims))]
    values = values.at[tuple(spot)].set(smallest)
    longest = dims.index(max(dims))
    spot[longest] = (spot[longest] + 1) % dims[longest]
    return values.at[tuple(spot)].set(largest)


def level_of(rng, extent, pieces, least, high):
    def one(position, shards_of):
        steps = jax.random.uniform(jax.random.fold_in(jax.random.fold_in(rng, 6), position), (shards_of,), jnp.float32, least / len(pieces), high / len(pieces))
        return jnp.repeat(jnp.exp(steps), extent[position] // shards_of).reshape((-1,) + (1,) * (len(extent) - position - 1))

    level = one(*pieces[0])
    for cut in pieces[1:]:
        level = level * one(*cut)
    return level


def skewed_wide(rng, dims, number_of, lean):
    weights = [min(1 << octave, number_of + 1 - (1 << octave)) * (1 << 20) // math.isqrt((1 << octave) ** lean) + 1 for octave in range((number_of + 1).bit_length()) if 1 << octave <= number_of]
    width = 1 + sum(weights) // (1 << 30)
    grid = np.cumsum(np.array([max(1, weight // width) for weight in weights]))
    lot = jax.random.randint(jax.random.fold_in(rng, 1), dims, 0, int(grid[len(weights) - 1]))
    start = jnp.left_shift(1, jnp.searchsorted(jnp.asarray(grid, jnp.int32), lot, side="right").astype(jnp.int32))
    rank = start - 1 + jax.random.randint(jax.random.fold_in(rng, 4), dims, 0, 1 << 30) % jnp.minimum(start, number_of + 1 - start)
    return jax.random.permutation(jax.random.fold_in(rng, 2), number_of)[rank].astype(jnp.int32)


def normal_values(rng, shape, width, reach, shards=(), held_as=jnp.bfloat16):
    gain = level_of(rng, shape, shards, -0.22, 0.18) if shards else 1.0
    array = jax.random.normal(rng, shape, jnp.float32) * width * gain
    return jnp.minimum(jnp.maximum(array, -reach), reach).astype(held_as)


def setup_inputs(seed: int = 0) -> dict:
    keys = jax.random.split(jax.random.key(seed), 5)
    queries_raw = normal_values(keys[0], (Q, D), 0.25, 1.5, ((0, 256),), jnp.float32)
    projection = normal_values(keys[1], (D, D), D ** -0.5, 0.21875, (), jnp.float32)
    passages = draw_passages(jax.random.fold_in(keys[4], 71), 0)
    positives = set_ends(skewed_wide(keys[3], (Q, POS), NP, 2), jax.random.fold_in(keys[3], 3), 0, NP - 1).astype(jnp.int32)
    return {"queries_raw": queries_raw, "projection": projection, "passages": passages, "positives": positives}


def reference(queries_raw, projection, passages, positives):
    hp = lax.Precision.HIGHEST
    projected = jnp.dot(queries_raw, projection, precision=hp, preferred_element_type=jnp.float32)
    query_emb = lax.optimization_barrier(projected.astype(jnp.bfloat16)).astype(jnp.float32)
    wide = passages.astype(jnp.float32)
    total = wide.shape[0]
    scale = 1.0 / (4.0 * total)
    block = 32

    def one_block(pair):
        qblock, pblock = pair
        scores = jnp.dot(qblock, wide.T, precision=hp, preferred_element_type=jnp.float32)
        pos_scores = jnp.take_along_axis(scores, pblock, axis=1)
        loss_sum = jnp.zeros((block,), jnp.float32)
        dsum = jnp.zeros_like(scores)
        pos_list = []
        for slot in range(POS):
            sig = jax.nn.sigmoid(scores - pos_scores[:, slot:slot + 1])
            loss_sum = loss_sum + jnp.sum(sig, axis=1)
            slope = sig * (1.0 - sig)
            dsum = dsum + slope
            pos_list.append(-jnp.sum(slope, axis=1))
        pos_grad = jnp.stack(pos_list, axis=1) * scale
        grad = dsum * scale
        row_ids = jnp.broadcast_to(jnp.arange(block, dtype=jnp.int32)[:, None], pblock.shape)
        grad = grad.at[row_ids, pblock].add(pos_grad)
        grad_b = lax.optimization_barrier(grad.astype(jnp.bfloat16)).astype(jnp.float32)
        query_grad = jnp.dot(grad_b, wide, precision=hp, preferred_element_type=jnp.float32)
        return query_grad, loss_sum * scale

    query_grad, loss = lax.map(one_block, (query_emb.reshape(-1, block, D), positives.reshape(-1, block, POS)))
    query_grad = query_grad.reshape(-1, D)
    loss = loss.reshape(-1)
    grad_raw = jnp.dot(query_grad, projection.T, precision=hp, preferred_element_type=jnp.float32)
    grad_projection = jnp.dot(queries_raw.T, query_grad, precision=hp, preferred_element_type=jnp.float32)
    return loss, grad_raw, grad_projection
```

```python
import jax
import jax.numpy as jnp
from jax import lax
from jax.sharding import Mesh, PartitionSpec as P

POS = 4
ALL = ("x", "z", "y", "c")
XY = ("x", "y")


def exchange(v, axes):
    return lax.all_to_all(v, axes, 0, 0, tiled=False)


def spread(v, axes):
    n = lax.axis_size(axes)
    return exchange(jnp.broadcast_to(v[None], (n,) + v.shape), axes)


def total(v):
    v = jnp.sum(spread(v, XY), axis=0)
    return jnp.sum(spread(v, "z"), axis=0)


def shards(queries_raw, projection, passages, positives):
    hp = lax.Precision.HIGHEST
    rows, dim = passages.shape
    own = queries_raw.shape[0]
    nz, nxy = lax.axis_size("z"), lax.axis_size(XY)
    plane = nz * own
    queries = nxy * plane
    scale = 1.0 / (4.0 * rows * nz * nxy)
    bf16 = jnp.bfloat16

    raw_all = lax.all_gather(queries_raw.astype(bf16), ALL, axis=0, tiled=True)

    projected = jnp.dot(queries_raw, projection, precision=hp, preferred_element_type=jnp.float32)
    ids = jnp.concatenate([positives >> 14, (positives >> 7) & 127, positives & 127], axis=1)
    ids = jnp.pad(ids, ((0, 0), (0, 128 - 3 * POS)))
    packet = jnp.concatenate([projected.astype(bf16), ids.astype(bf16)], axis=1)
    packet = spread(packet, "z").reshape(plane, dim + 128)
    packet = spread(packet, XY).reshape(queries, dim + 128)
    all_emb = packet[:, :dim]
    ids = packet[:, dim : dim + 3 * POS].astype(jnp.float32).astype(jnp.int32)
    all_pos = (ids[:, :POS] << 14) + (ids[:, POS : 2 * POS] << 7) + ids[:, 2 * POS :]

    shard = (lax.axis_index("x") * nz + lax.axis_index("z")) * lax.axis_size("y") + lax.axis_index("y")
    local_pos = all_pos - shard * rows
    scores = lax.dot_general(
        all_emb, passages, (((1,), (1,)), ((), ())), preferred_element_type=jnp.float32
    )
    columns = jnp.arange(rows, dtype=jnp.int32)[None, :]
    owned = [local_pos[:, slot : slot + 1] == columns for slot in range(POS)]
    partial_pos = jnp.stack(
        [jnp.sum(jnp.where(owned[slot], scores, 0.0), axis=1) for slot in range(POS)], axis=0
    )
    pos_scores = total(partial_pos).T
    loss_part = jnp.zeros((queries,), jnp.float32)
    slope_sum = jnp.zeros_like(scores)
    parts = []
    for slot in range(POS):
        sig = jax.nn.sigmoid(scores - pos_scores[:, slot : slot + 1])
        loss_part = loss_part + jnp.sum(sig, axis=1)
        slope = sig * (1.0 - sig)
        slope_sum = slope_sum + slope
        parts.append(-jnp.sum(slope, axis=1))
    sums = total(jnp.stack(parts + [loss_part], axis=0) * scale)
    pos_grad = sums[:POS].T
    grad = slope_sum * scale
    for slot in range(POS):
        grad = grad + jnp.where(owned[slot], pos_grad[:, slot : slot + 1], 0.0)
    part = jnp.dot(grad.astype(bf16), passages, preferred_element_type=jnp.float32)

    part = exchange(part.astype(bf16).reshape(nxy, plane, dim), XY)
    part = jnp.sum(part.astype(jnp.float32), axis=0).astype(bf16)
    summed = jnp.sum(spread(part, "z").astype(jnp.float32), axis=0)

    home = lax.axis_index("z") * own
    query_grad = lax.dynamic_slice_in_dim(summed, home, own, 0)
    grad_raw = jnp.dot(query_grad, projection.T, precision=hp, preferred_element_type=jnp.float32)
    first = lax.axis_index(XY) * plane + home
    loss = lax.dynamic_slice_in_dim(sums[POS], first, own, 0)

    mine = spread(summed.astype(bf16), XY).reshape(queries, dim)
    other = lax.ppermute(mine, "c", [(0, 1), (1, 0)])
    even = lax.axis_index("c") == 0
    grads = jnp.concatenate([jnp.where(even, mine, other), jnp.where(even, other, mine)], axis=0)
    sizes = [lax.axis_size(a) for a in ALL]
    raw = raw_all.reshape(*sizes, own, dim).transpose(3, 0, 2, 1, 4, 5).reshape(2 * queries, dim)
    grad_projection = lax.dot_general(
        raw, grads, (((0,), (0,)), ((), ())), preferred_element_type=jnp.float32
    )
    return (loss, grad_raw, grad_projection)


def solution(mesh):
    axes = Mesh(mesh.devices.reshape(4, 8, 4, 2), ALL)
    in_specs = (P(ALL, None), P(), P(("x", "z", "y"), None), P(ALL, None))
    out_specs = (P(ALL), P(ALL, None), P())
    return jax.shard_map(shards, mesh=axes, in_specs=in_specs, out_specs=out_specs, check_vma=False)
```

```python
import functools

import jax
import jax.numpy as jnp
from jax import lax
from jax.experimental import pallas as pl
from jax.experimental.pallas import tpu as pltpu
from jax.sharding import Mesh, PartitionSpec as P

POS = 4
ALL = ("x", "z", "y", "c")
XY = ("x", "y")
LANES = 128
CLAMP = 80.0
BF16 = jnp.bfloat16
F32 = jnp.float32


def params(*semantics):
    return pltpu.CompilerParams(dimension_semantics=semantics or None, vmem_limit_bytes=50 * 1024 * 1024)


def columns_to_rows(columns):
    rows = columns[0].shape[0]
    lane = lax.broadcasted_iota(jnp.int32, (rows, LANES), 1)
    table = jnp.zeros((rows, LANES), F32)
    for k, column in enumerate(columns):
        table = jnp.where(lane == k, column, table)
    return table.T[:8]


def rows_to_columns(rows):
    wide = jnp.concatenate([rows, jnp.zeros((LANES - 8, rows.shape[1]), F32)], axis=0)
    return wide.T


def score_kernel(packet_ref, passages_ref, ids_ref, scores_ref, pos_ref, chunk, found):
    step = pl.program_id(0)
    groups, _, dim = packet_ref.shape
    queries, width = scores_ref.shape

    @pl.when(step == 0)
    def _():
        for k in range(POS):
            ids = ids_ref[:, k : k + 1]
            chunk[k] = jnp.broadcast_to(ids >> 7, (queries, LANES))
        found[...] = jnp.zeros_like(found)

    emb = packet_ref[:, : queries // groups, :].reshape(queries, dim)
    scores = lax.dot_general(
        emb, passages_ref[...], (((1,), (1,)), ((), ())), preferred_element_type=F32
    )
    scores_ref[...] = scores
    first = step * (width // LANES)
    for tile in range(queries // 8):
        rows = slice(tile * 8, tile * 8 + 8)
        for k in range(POS):
            want = chunk[k, rows, :] - first
            best = found[k, rows, :]
            for c in range(width // LANES):
                best = jnp.where(want == c, scores[rows, c * LANES : (c + 1) * LANES], best)
            found[k, rows, :] = best

    @pl.when(step == pl.num_programs(0) - 1)
    def _():
        lane = lax.broadcasted_iota(jnp.int32, (queries, LANES), 1)
        columns = []
        for k in range(POS):
            hit = lane == (ids_ref[:, k : k + 1] & (LANES - 1))
            columns.append(jnp.sum(jnp.where(hit, found[k], 0.0), axis=1, keepdims=True))
        rows = columns_to_rows(columns)
        for g in range(pos_ref.shape[0]):
            pos_ref[g] = rows


def score_call(packet, passages, ids, queries, block=512):
    rows, dim = passages.shape
    groups = packet.shape[0]
    return pl.pallas_call(
        score_kernel,
        grid=(rows // block,),
        in_specs=[
            pl.BlockSpec(packet.shape, lambda j: (0, 0, 0)),
            pl.BlockSpec((block, dim), lambda j: (j, 0)),
            pl.BlockSpec(ids.shape, lambda j: (0, 0)),
        ],
        out_specs=[
            pl.BlockSpec((queries, block), lambda j: (0, j)),
            pl.BlockSpec((groups, 8, queries), lambda j: (0, 0, 0)),
        ],
        out_shape=[
            jax.ShapeDtypeStruct((queries, rows), F32),
            jax.ShapeDtypeStruct((groups, 8, queries), F32),
        ],
        scratch_shapes=[
            pltpu.VMEM((POS, queries, LANES), jnp.int32),
            pltpu.VMEM((POS, queries, LANES), F32),
        ],
        compiler_params=params("arbitrary"),
        cost_estimate=pl.CostEstimate(
            flops=2 * queries * rows * dim, bytes_accessed=rows * dim * 2 + queries * rows * 4, transcendentals=0
        ),
        name="score",
    )(packet, passages, ids)


def sigmoid_kernel(scale, pos_ref, scores_ref, slopes_ref, sums_ref, pos, sums):
    step = pl.program_id(0)
    block, width = scores_ref.shape

    @pl.when(step == 0)
    def _():
        rows = pos_ref[0]
        for g in range(1, pos_ref.shape[0]):
            rows = rows + pos_ref[g]
        pos[...] = rows_to_columns(rows)

    def tile(t, carry):
        at = pl.multiple_of(t * 8, 8)
        own = pl.ds(pl.multiple_of(step * block + t * 8, 8), 8)
        columns = pos[own, :]
        p = [jnp.broadcast_to(columns[:, k : k + 1], (8, LANES)) for k in range(POS)]
        slope_acc = [jnp.zeros((8, LANES), F32) for _ in range(POS)]
        loss_acc = jnp.zeros((8, LANES), F32)
        for c in range(width // LANES):
            s = scores_ref[pl.ds(at, 8), c * LANES : (c + 1) * LANES]
            both = None
            for k in range(POS):
                e = jnp.exp(jnp.minimum(p[k] - s, CLAMP))
                sig = 1.0 / (1.0 + e)
                slope = e * (sig * sig)
                loss_acc = loss_acc + sig
                slope_acc[k] = slope_acc[k] + slope
                both = slope if both is None else both + slope
            slopes_ref[pl.ds(at, 8), c * LANES : (c + 1) * LANES] = both * scale
        for k in range(POS):
            sums[k, own, :] = slope_acc[k]
        sums[POS, own, :] = loss_acc
        return carry

    lax.fori_loop(0, block // 8, tile, 0)

    @pl.when(step == pl.num_programs(0) - 1)
    def _():
        columns = [jnp.sum(sums[k], axis=1, keepdims=True) * (scale if k == POS else -scale) for k in range(POS + 1)]
        rows = columns_to_rows(columns)
        for g in range(sums_ref.shape[0]):
            sums_ref[g] = rows


def sigmoid_call(pos, scores, scale, groups, block=64):
    queries, width = scores.shape
    return pl.pallas_call(
        functools.partial(sigmoid_kernel, scale),
        grid=(queries // block,),
        in_specs=[
            pl.BlockSpec(pos.shape, lambda j: (0, 0, 0)),
            pl.BlockSpec((block, width), lambda j: (j, 0)),
        ],
        out_specs=[
            pl.BlockSpec((block, width), lambda j: (j, 0)),
            pl.BlockSpec((groups, 8, queries), lambda j: (0, 0, 0)),
        ],
        out_shape=[
            jax.ShapeDtypeStruct((queries, width), F32),
            jax.ShapeDtypeStruct((groups, 8, queries), F32),
        ],
        scratch_shapes=[
            pltpu.VMEM((queries, LANES), F32),
            pltpu.VMEM((POS + 1, queries, LANES), F32),
        ],
        compiler_params=params("arbitrary"),
        cost_estimate=pl.CostEstimate(
            flops=40 * queries * width, bytes_accessed=queries * width * 8, transcendentals=8 * queries * width
        ),
        name="sigmoid",
    )(pos, scores)


def grad_kernel(sums_ref, slopes_ref, passages_ref, ids_ref, part_ref, total_ref, ids, grads, left, acc):
    step = pl.program_id(0)
    queries, width = slopes_ref.shape

    @pl.when(step == 0)
    def _():
        rows = sums_ref[0]
        for g in range(1, sums_ref.shape[0]):
            rows = rows + sums_ref[g]
        total_ref[...] = rows
        columns = rows_to_columns(rows)
        for k in range(POS):
            ids[k] = jnp.broadcast_to(ids_ref[:, k : k + 1], (queries, LANES))
            grads[k] = jnp.broadcast_to(columns[:, k : k + 1], (queries, LANES))

    lane = lax.broadcasted_iota(jnp.int32, (16, LANES), 1)
    for tile in range(queries // 16):
        rows = slice(tile * 16, tile * 16 + 16)
        want = [ids[k, rows, :] - step * width - lane for k in range(POS)]
        give = [grads[k, rows, :] for k in range(POS)]
        for c in range(width // LANES):
            g = slopes_ref[rows, c * LANES : (c + 1) * LANES]
            for k in range(POS):
                g = g + jnp.where(want[k] == c * LANES, give[k], 0.0)
            left[rows, c * LANES : (c + 1) * LANES] = g.astype(BF16)
    product = jnp.dot(left[...], passages_ref[...], preferred_element_type=F32)

    @pl.when(step == 0)
    def _():
        acc[...] = product

    @pl.when(step > 0)
    def _():
        acc[...] += product

    @pl.when(step == pl.num_programs(0) - 1)
    def _():
        part_ref[...] = acc[...].astype(BF16).reshape(part_ref.shape)


def grad_call(sums, slopes, passages, ids, groups, block=1024):
    rows, dim = passages.shape
    queries = slopes.shape[0]
    return pl.pallas_call(
        grad_kernel,
        grid=(rows // block,),
        in_specs=[
            pl.BlockSpec(sums.shape, lambda j: (0, 0, 0)),
            pl.BlockSpec((queries, block), lambda j: (0, j)),
            pl.BlockSpec((block, dim), lambda j: (j, 0)),
            pl.BlockSpec(ids.shape, lambda j: (0, 0)),
        ],
        out_specs=[
            pl.BlockSpec((groups, queries // groups, dim), lambda j: (0, 0, 0)),
            pl.BlockSpec((8, queries), lambda j: (0, 0)),
        ],
        out_shape=[
            jax.ShapeDtypeStruct((groups, queries // groups, dim), BF16),
            jax.ShapeDtypeStruct((8, queries), F32),
        ],
        scratch_shapes=[
            pltpu.VMEM((POS, queries, LANES), jnp.int32),
            pltpu.VMEM((POS, queries, LANES), F32),
            pltpu.VMEM((queries, block), BF16),
            pltpu.VMEM((queries, dim), F32),
        ],
        compiler_params=params("arbitrary"),
        cost_estimate=pl.CostEstimate(
            flops=2 * queries * rows * dim, bytes_accessed=rows * dim * 2 + queries * rows * 4, transcendentals=0
        ),
        name="grad",
    )(sums, slopes, passages, ids)


def fold_kernel(parts_ref, out_ref):
    acc = parts_ref[0].astype(F32)
    for g in range(1, parts_ref.shape[0]):
        acc = acc + parts_ref[g].astype(F32)
    for g in range(out_ref.shape[0]):
        out_ref[g] = acc.astype(out_ref.dtype)


def fold_call(parts, n):
    return pl.pallas_call(
        fold_kernel,
        out_shape=jax.ShapeDtypeStruct((n,) + parts.shape[1:], parts.dtype),
        compiler_params=params(),
        name="fold",
    )(parts)


def fold_both_kernel(parts_ref, out_ref, sum_ref):
    acc = parts_ref[0].astype(F32)
    for g in range(1, parts_ref.shape[0]):
        acc = acc + parts_ref[g].astype(F32)
    sum_ref[...] = acc
    for g in range(out_ref.shape[0]):
        out_ref[g] = acc.astype(out_ref.dtype)


def fold_both_call(parts, n):
    return pl.pallas_call(
        fold_both_kernel,
        out_shape=[
            jax.ShapeDtypeStruct((n,) + parts.shape[1:], parts.dtype),
            jax.ShapeDtypeStruct(parts.shape[1:], F32),
        ],
        compiler_params=params(),
        name="fold_both",
    )(parts)


def final_kernel(core_ref, packet_ref, raw_ref, mine_ref, other_ref, out_ref):
    groups, plane, dim = mine_ref.shape
    queries = groups * plane

    def term(raw, grads):
        return lax.dot_general(raw, grads, (((0,), (0,)), ((), ())), preferred_element_type=F32)

    def both(first, second):
        out_ref[...] = term(*first)
        out_ref[...] += term(*second)

    own = (packet_ref[:, plane : 2 * plane, :].reshape(queries, dim), mine_ref[...].reshape(queries, dim))
    peer = (raw_ref[...].reshape(queries, dim), other_ref[...].reshape(queries, dim))

    @pl.when(core_ref[0] == 0)
    def _():
        both(own, peer)

    @pl.when(core_ref[0] != 0)
    def _():
        both(peer, own)


def final_call(core, packet, raw, mine, other):
    dim = mine.shape[-1]
    return pl.pallas_call(
        final_kernel,
        in_specs=[pl.BlockSpec(memory_space=pltpu.SMEM)] + [pl.BlockSpec(memory_space=pltpu.VMEM)] * 4,
        out_shape=jax.ShapeDtypeStruct((dim, dim), F32),
        compiler_params=params(),
        name="final",
    )(core, packet, raw, mine, other)


def exchange(v, axes):
    return lax.all_to_all(v, axes, 0, 0, tiled=False)


def spread(v, axes):
    return exchange(jnp.broadcast_to(v[None], (lax.axis_size(axes),) + v.shape), axes)


def shards(queries_raw, projection, passages, positives):
    hp = lax.Precision.HIGHEST
    rows, dim = passages.shape
    own = queries_raw.shape[0]
    nz, nxy = lax.axis_size("z"), lax.axis_size(XY)
    plane = nz * own
    queries = nxy * plane
    scale = 1.0 / (4.0 * rows * nz * nxy)
    core = lax.axis_index("c")
    swap = [(0, 1), (1, 0)]

    projected = jnp.dot(queries_raw, projection, precision=hp, preferred_element_type=F32)
    ids = jnp.concatenate([positives >> 14, (positives >> 7) & 127, positives & 127], axis=1)
    ids = jnp.pad(ids, ((0, 0), (0, LANES - 3 * POS)))
    packet = jnp.concatenate([projected.astype(BF16), queries_raw.astype(BF16), ids.astype(BF16)], axis=1)
    packet = spread(packet, "z").reshape(plane, 2 * dim + LANES)
    ids = packet[:, 2 * dim : 2 * dim + 3 * POS].reshape(1, 3 * POS * plane)
    ids = jnp.pad(ids, ((0, 7), (0, dim - 3 * POS * plane)))
    packet = jnp.concatenate([packet[:, :dim], packet[:, dim : 2 * dim], ids], axis=0)
    packet = spread(packet, XY)

    raw_other = lax.ppermute(packet[:, plane : 2 * plane, :], "c", swap)
    ids = packet[:, 2 * plane, : 3 * POS * plane].reshape(queries, 3 * POS).astype(F32).astype(jnp.int32)
    all_pos = (ids[:, :POS] << 14) + (ids[:, POS : 2 * POS] << 7) + ids[:, 2 * POS :]
    shard = (lax.axis_index("x") * nz + lax.axis_index("z")) * lax.axis_size("y") + lax.axis_index("y")
    local_pos = all_pos - shard * rows

    scores, pos = score_call(packet, passages, local_pos, queries)
    pos = exchange(fold_call(exchange(pos, XY), nz), "z")
    slopes, sums = sigmoid_call(pos, scores, scale, nxy)
    sums = exchange(fold_call(exchange(sums, XY), nz), "z")
    part, sums = grad_call(sums, slopes, passages, local_pos, nxy)

    part = exchange(fold_call(exchange(part, XY), nz), "z")
    part, summed = fold_both_call(part, nxy)
    mine = exchange(part, XY)
    other = lax.ppermute(mine, "c", swap)

    home = lax.axis_index("z") * own
    query_grad = lax.dynamic_slice_in_dim(summed, home, own, 0)
    grad_raw = jnp.dot(query_grad, projection.T, precision=hp, preferred_element_type=F32)
    first = lax.axis_index(XY) * plane + home
    loss = lax.dynamic_slice_in_dim(sums[POS], first, own, 0)
    grad_projection = final_call(core.reshape(1), packet, raw_other, mine, other)
    return (loss, grad_raw, grad_projection)


def solution(mesh):
    axes = Mesh(mesh.devices.reshape(4, 8, 4, 2), ALL)
    in_specs = (P(ALL, None), P(), P(("x", "z", "y"), None), P(ALL, None))
    out_specs = (P(ALL), P(ALL, None), P())
    return jax.shard_map(shards, mesh=axes, in_specs=in_specs, out_specs=out_specs, check_vma=False)
```

```python
import functools

import jax
import jax.numpy as jnp
from jax import lax
from jax.experimental import pallas as pl
from jax.experimental.pallas import tpu as pltpu
from jax.sharding import Mesh, PartitionSpec as P

POS = 4
ALL = ("x", "z", "y", "c")
XY = ("x", "y")
LANES = 128
BF16 = jnp.bfloat16
F32 = jnp.float32


def params():
    return pltpu.CompilerParams(vmem_limit_bytes=26 * 1024 * 1024)


def columns_to_rows(columns):
    rows = columns[0].shape[0]
    lane = lax.broadcasted_iota(jnp.int32, (rows, LANES), 1)
    table = jnp.zeros((rows, LANES), F32)
    for k, column in enumerate(columns):
        table = jnp.where(lane == k, column, table)
    return table.T[:8]


def rows_to_columns(rows):
    wide = jnp.concatenate([rows, jnp.zeros((LANES - 8, rows.shape[1]), F32)], axis=0)
    return wide.T


def score_kernel(shard_ref, packet_ref, passages_ref, scores_ref, pos_ref, ids_ref, chunk, found):
    groups, plane, _ = packet_ref.shape
    rows, dim = passages_ref.shape
    queries = groups * plane
    width = 512

    codes = packet_ref[:, :, 2 * dim :].reshape(queries, LANES).astype(F32).astype(jnp.int32)
    for k in range(POS):
        high, mid, low = (codes[:, k + POS * part : k + POS * part + 1] for part in range(3))
        ids = (high << 14) + (mid << 7) + low - shard_ref[0] * rows
        ids = jnp.broadcast_to(ids, (queries, LANES))
        ids_ref[k] = ids
        chunk[k] = ids >> 7
    found[...] = jnp.zeros_like(found)

    def product(j):
        at = pl.multiple_of(j * width, width)
        emb = packet_ref[:, :, :dim].reshape(queries, dim)
        scores_ref[:, pl.ds(at, width)] = lax.dot_general(
            emb, passages_ref[pl.ds(at, width), :], (((1,), (1,)), ((), ())), preferred_element_type=F32
        )

    def extract(j):
        first = j * (width // LANES)
        for tile in range(queries // 8):
            here = slice(tile * 8, tile * 8 + 8)
            scores = [
                scores_ref[here, pl.ds(pl.multiple_of(j * width + c * LANES, LANES), LANES)]
                for c in range(width // LANES)
            ]
            for k in range(POS):
                want = chunk[k, here, :] - first
                best = found[k, here, :]
                for c, s in enumerate(scores):
                    best = jnp.where(want == c, s, best)
                found[k, here, :] = best

    def step(j, carry):
        extract(j - 1)
        product(j)
        return carry

    steps = rows // width
    product(0)
    lax.fori_loop(1, steps, step, 0)
    extract(steps - 1)

    lane = lax.broadcasted_iota(jnp.int32, (queries, LANES), 1)
    columns = []
    for k in range(POS):
        hit = lane == (ids_ref[k] & (LANES - 1))
        columns.append(jnp.sum(jnp.where(hit, found[k], 0.0), axis=1, keepdims=True))
    table = columns_to_rows(columns)
    for g in range(groups):
        pos_ref[g] = table


def score_call(shard, packet, passages):
    rows, dim = passages.shape
    groups, plane, _ = packet.shape
    queries = groups * plane
    return pl.pallas_call(
        score_kernel,
        in_specs=[pl.BlockSpec(memory_space=pltpu.SMEM)] + [pl.BlockSpec(memory_space=pltpu.VMEM)] * 2,
        out_shape=[
            jax.ShapeDtypeStruct((queries, rows), F32),
            jax.ShapeDtypeStruct((groups, 8, queries), F32),
            jax.ShapeDtypeStruct((POS, queries, LANES), jnp.int32),
        ],
        scratch_shapes=[
            pltpu.VMEM((POS, queries, LANES), jnp.int32),
            pltpu.VMEM((POS, queries, LANES), F32),
        ],
        compiler_params=params(),
        cost_estimate=pl.CostEstimate(
            flops=4 * queries * rows * dim, bytes_accessed=rows * dim * 2 + queries * rows * 4, transcendentals=0
        ),
        name="score",
    )(shard, packet, passages)


def sigmoid_kernel(scale, pos_ref, scores_ref, slopes_ref, sums_ref, pos, sums):
    queries, width = scores_ref.shape
    size = 16
    rows = pos_ref[0]
    for g in range(1, pos_ref.shape[0]):
        rows = rows + pos_ref[g]
    pos[...] = rows_to_columns(rows)

    def tile(t, carry):
        at = pl.ds(pl.multiple_of(t * size, size), size)
        columns = pos[at, :]
        p = [jnp.broadcast_to(columns[:, k : k + 1], (size, LANES)) for k in range(POS)]
        slope_acc = [jnp.zeros((size, LANES), F32) for _ in range(POS)]
        loss_acc = jnp.zeros((size, LANES), F32)
        for c in range(width // LANES):
            s = scores_ref[at, c * LANES : (c + 1) * LANES]
            sigs = [jax.nn.sigmoid(s - p[k]) for k in range(POS)]
            slopes = [sig * (1.0 - sig) for sig in sigs]
            loss_acc = loss_acc + ((sigs[0] + sigs[1]) + (sigs[2] + sigs[3]))
            slope_acc = [slope_acc[k] + slopes[k] for k in range(POS)]
            both = (slopes[0] + slopes[1]) + (slopes[2] + slopes[3])
            slopes_ref[at, c * LANES : (c + 1) * LANES] = both * scale
        for k in range(POS):
            sums[k, at, :] = slope_acc[k]
        sums[POS, at, :] = loss_acc
        return carry

    lax.fori_loop(0, queries // size, tile, 0)
    columns = [jnp.sum(sums[k], axis=1, keepdims=True) * (scale if k == POS else -scale) for k in range(POS + 1)]
    rows = columns_to_rows(columns)
    for g in range(sums_ref.shape[0]):
        sums_ref[g] = rows


def sigmoid_call(pos, scores, scale, groups):
    queries, width = scores.shape
    return pl.pallas_call(
        functools.partial(sigmoid_kernel, scale),
        in_specs=[pl.BlockSpec(memory_space=pltpu.VMEM)] * 2,
        out_shape=[
            jax.ShapeDtypeStruct((queries, width), F32),
            jax.ShapeDtypeStruct((groups, 8, queries), F32),
        ],
        scratch_shapes=[
            pltpu.VMEM((queries, LANES), F32),
            pltpu.VMEM((POS + 1, queries, LANES), F32),
        ],
        compiler_params=params(),
        cost_estimate=pl.CostEstimate(
            flops=40 * queries * width, bytes_accessed=queries * width * 8, transcendentals=8 * queries * width
        ),
        name="sigmoid",
    )(pos, scores)


def grad_kernel(sums_ref, slopes_ref, passages_ref, ids_ref, part_ref, total_ref, grads, left_a, left_b, acc):
    queries, rows = slopes_ref.shape
    width = left_a.shape[1]
    table = sums_ref[0]
    for g in range(1, sums_ref.shape[0]):
        table = table + sums_ref[g]
    total_ref[...] = table
    columns = rows_to_columns(table)
    for k in range(POS):
        give = columns[:, k : k + 1]
        for other in range(POS):
            if other != k:
                same = ids_ref[k] == ids_ref[other]
                give = give + jnp.where(same, columns[:, other : other + 1], 0.0)
        grads[k] = jnp.broadcast_to(give, (queries, LANES))

    def build(left, j):
        lane = lax.broadcasted_iota(jnp.int32, (16, LANES), 1) + j * width
        for tile in range(queries // 16):
            here = slice(tile * 16, tile * 16 + 16)
            want = [ids_ref[k, here, :] - lane for k in range(POS)]
            give = [grads[k, here, :] for k in range(POS)]
            for c in range(width // LANES):
                extra = jnp.zeros((16, LANES), F32)
                for k in range(POS):
                    extra = jnp.where(want[k] == c * LANES, give[k], extra)
                at = pl.ds(pl.multiple_of(j * width + c * LANES, LANES), LANES)
                left[here, c * LANES : (c + 1) * LANES] = (slopes_ref[here, at] + extra).astype(BF16)

    def product(left, j):
        block = passages_ref[pl.ds(pl.multiple_of(j * width, width), width), :]
        return jnp.dot(left[...], block, preferred_element_type=F32)

    steps = rows // width
    build(left_a, 0)
    for j in range(steps):
        now, later = (left_a, left_b) if j % 2 == 0 else (left_b, left_a)
        if j + 1 < steps:
            build(later, j + 1)
        term = product(now, j)
        if j == 0:
            acc[...] = term
        elif j + 1 < steps:
            acc[...] += term
        else:
            part_ref[...] = (acc[...] + term).astype(BF16).reshape(part_ref.shape)


def grad_call(sums, slopes, passages, ids, groups, block=1024):
    rows, dim = passages.shape
    queries = slopes.shape[0]
    return pl.pallas_call(
        grad_kernel,
        in_specs=[pl.BlockSpec(memory_space=pltpu.VMEM)] * 4,
        out_shape=[
            jax.ShapeDtypeStruct((groups, queries // groups, dim), BF16),
            jax.ShapeDtypeStruct((8, queries), F32),
        ],
        scratch_shapes=[
            pltpu.VMEM((POS, queries, LANES), F32),
            pltpu.VMEM((queries, block), BF16),
            pltpu.VMEM((queries, block), BF16),
            pltpu.VMEM((queries, dim), F32),
        ],
        compiler_params=params(),
        cost_estimate=pl.CostEstimate(
            flops=4 * queries * rows * dim, bytes_accessed=rows * dim * 2 + queries * rows * 4, transcendentals=0
        ),
        name="grad",
    )(sums, slopes, passages, ids)


def fold_kernel(parts_ref, out_ref):
    acc = parts_ref[0].astype(F32)
    for g in range(1, parts_ref.shape[0]):
        acc = acc + parts_ref[g].astype(F32)
    for g in range(out_ref.shape[0]):
        out_ref[g] = acc.astype(out_ref.dtype)


def fold_call(parts, n):
    return pl.pallas_call(
        fold_kernel,
        out_shape=jax.ShapeDtypeStruct((n,) + parts.shape[1:], parts.dtype),
        compiler_params=params(),
        name="fold",
    )(parts)


def fold_both_kernel(parts_ref, out_ref, sum_ref):
    acc = parts_ref[0].astype(F32)
    for g in range(1, parts_ref.shape[0]):
        acc = acc + parts_ref[g].astype(F32)
    sum_ref[...] = acc
    for g in range(out_ref.shape[0]):
        out_ref[g] = acc.astype(out_ref.dtype)


def fold_both_call(parts, n):
    return pl.pallas_call(
        fold_both_kernel,
        out_shape=[
            jax.ShapeDtypeStruct((n,) + parts.shape[1:], parts.dtype),
            jax.ShapeDtypeStruct(parts.shape[1:], F32),
        ],
        compiler_params=params(),
        name="fold_both",
    )(parts)


def final_kernel(core_ref, packet_ref, peer_ref, mine_ref, other_ref, out_ref):
    groups, plane, dim = mine_ref.shape
    queries = groups * plane

    def term(raw, grads):
        return lax.dot_general(raw, grads, (((0,), (0,)), ((), ())), preferred_element_type=F32)

    def both(first, second):
        out_ref[...] = term(*first)
        out_ref[...] += term(*second)

    own = (packet_ref[:, :, dim : 2 * dim].reshape(queries, dim), mine_ref[...].reshape(queries, dim))
    peer = (peer_ref[:, :, dim : 2 * dim].reshape(queries, dim), other_ref[...].reshape(queries, dim))

    @pl.when(core_ref[0] == 0)
    def _():
        both(own, peer)

    @pl.when(core_ref[0] != 0)
    def _():
        both(peer, own)


def final_call(core, packet, peer, mine, other):
    dim = mine.shape[-1]
    return pl.pallas_call(
        final_kernel,
        in_specs=[pl.BlockSpec(memory_space=pltpu.SMEM)] + [pl.BlockSpec(memory_space=pltpu.VMEM)] * 4,
        out_shape=jax.ShapeDtypeStruct((dim, dim), F32),
        compiler_params=params(),
        name="final",
    )(core, packet, peer, mine, other)


def exchange(v, axes):
    return lax.all_to_all(v, axes, 0, 0, tiled=False)


def spread(v, axes):
    return exchange(jnp.broadcast_to(v[None], (lax.axis_size(axes),) + v.shape), axes)


def shards(queries_raw, projection, passages, positives):
    hp = lax.Precision.HIGHEST
    rows, dim = passages.shape
    own = queries_raw.shape[0]
    nz, nxy = lax.axis_size("z"), lax.axis_size(XY)
    plane = nz * own
    scale = 1.0 / (4.0 * rows * nz * nxy)
    core = lax.axis_index("c")
    swap = [(0, 1), (1, 0)]

    projected = jnp.dot(queries_raw, projection, precision=hp, preferred_element_type=F32)
    ids = jnp.concatenate([positives >> 14, (positives >> 7) & 127, positives & 127], axis=1)
    ids = jnp.pad(ids, ((0, 0), (0, LANES - 3 * POS)))
    packet = jnp.concatenate([projected.astype(BF16), queries_raw.astype(BF16), ids.astype(BF16)], axis=1)
    shard = (lax.axis_index("x") * nz + lax.axis_index("z")) * lax.axis_size("y") + lax.axis_index("y")
    packet, shard = lax.optimization_barrier((packet, shard))
    packet = spread(packet, "z").reshape(plane, 2 * dim + LANES)
    packet = spread(packet, XY)
    peer = lax.ppermute(packet, "c", swap)

    scores, pos, local_pos = score_call(shard.reshape(1), packet, passages)
    pos = exchange(fold_call(exchange(pos, XY), nz), "z")
    pos, peer = lax.optimization_barrier((pos, peer))
    slopes, sums = sigmoid_call(pos, scores, scale, nxy)
    sums = exchange(fold_call(exchange(sums, XY), nz), "z")
    part, sums = grad_call(sums, slopes, passages, local_pos, nxy)

    part = exchange(fold_call(exchange(part, XY), nz), "z")
    part, summed = fold_both_call(part, nxy)
    mine = exchange(part, XY)
    other = lax.ppermute(mine, "c", swap)

    home = lax.axis_index("z") * own
    query_grad = lax.dynamic_slice_in_dim(summed, home, own, 0)
    grad_raw = jnp.dot(query_grad, projection.T, precision=hp, preferred_element_type=F32)
    first = lax.axis_index(XY) * plane + home
    loss = lax.dynamic_slice_in_dim(sums[POS], first, own, 0)
    grad_projection = final_call(core.reshape(1), packet, peer, mine, other)
    return (loss, grad_raw, grad_projection)


def solution(mesh):
    axes = Mesh(mesh.devices.reshape(4, 8, 4, 2), ALL)
    in_specs = (P(ALL, None), P(), P(("x", "z", "y"), None), P(ALL, None))
    out_specs = (P(ALL), P(ALL, None), P())
    return jax.shard_map(shards, mesh=axes, in_specs=in_specs, out_specs=out_specs, check_vma=False)
```

```python
import functools

import jax
import jax.numpy as jnp
from jax import lax
from jax.experimental import pallas as pl
from jax.experimental.pallas import tpu as pltpu
from jax.sharding import Mesh, PartitionSpec as P

POS = 4
ALL = ("x", "z", "y", "c")
XY = ("x", "y")
LANES = 128
BF16 = jnp.bfloat16
F32 = jnp.float32


def params(mib):
    return pltpu.CompilerParams(vmem_limit_bytes=mib * 1024 * 1024)


def passage_copies(far, near, sems):
    width = near.shape[0] // sems.shape[0]

    def copy(j):
        at = pl.ds(pl.multiple_of(j * width, width), width)
        return pltpu.make_async_copy(far.at[at, :], near.at[at, :], sems.at[j])

    return copy


def in_three(x):
    high = x.astype(BF16).astype(F32)
    rest = x - high
    mid = rest.astype(BF16).astype(F32)
    return high, mid, rest - mid


def columns_to_rows(columns):
    rows = columns[0].shape[0]
    lane = lax.broadcasted_iota(jnp.int32, (rows, LANES), 1)
    table = jnp.zeros((rows, LANES), F32)
    for k, column in enumerate(columns):
        table = jnp.where(lane == k, column, table)
    return table.T[:8]


def rows_to_columns(rows):
    wide = jnp.concatenate([rows, jnp.zeros((LANES - 8, rows.shape[1]), F32)], axis=0)
    return wide.T


def score_kernel(shard_ref, packet_ref, raw_ref, passages_hbm, scores_ref, note_ref, ids_ref, chunk, found, passages, sems):
    groups, plane, _ = packet_ref.shape
    rows, dim = passages.shape
    queries = groups * plane
    steps = sems.shape[0]
    width = rows // steps
    copy = passage_copies(passages_hbm, passages, sems)
    for j in range(steps):
        copy(j).start()

    codes = packet_ref[:, :, dim:].reshape(queries, LANES).astype(F32).astype(jnp.int32)
    for k in range(POS):
        high, mid, low = (codes[:, k + POS * part : k + POS * part + 1] for part in range(3))
        ids = (high << 14) + (mid << 7) + low - shard_ref[0] * rows
        ids = jnp.broadcast_to(ids, (queries, LANES))
        ids_ref[k] = ids
        chunk[k] = ids >> 7
    found[...] = jnp.zeros_like(found)

    def product(j):
        copy(j).wait()
        at = pl.multiple_of(j * width, width)
        emb = packet_ref[:, :, :dim].reshape(queries, dim)
        scores_ref[:, pl.ds(at, width)] = lax.dot_general(
            emb, passages[pl.ds(at, width), :], (((1,), (1,)), ((), ())), preferred_element_type=F32
        )

    def extract(j):
        first = j * (width // LANES)
        for tile in range(queries // 8):
            here = slice(tile * 8, tile * 8 + 8)
            scores = [
                scores_ref[here, pl.ds(pl.multiple_of(j * width + c * LANES, LANES), LANES)]
                for c in range(width // LANES)
            ]
            for k in range(POS):
                want = chunk[k, here, :] - first
                best = found[k, here, :]
                for c, s in enumerate(scores):
                    best = jnp.where(want == c, s, best)
                found[k, here, :] = best

    def step(j, carry):
        extract(j - 1)
        product(j)
        return carry

    product(0)
    lax.fori_loop(1, steps, step, 0)
    extract(steps - 1)

    lane = lax.broadcasted_iota(jnp.int32, (queries, LANES), 1)
    columns = []
    for k in range(POS):
        hit = lane == (ids_ref[k] & (LANES - 1))
        columns.append(jnp.sum(jnp.where(hit, found[k], 0.0), axis=1, keepdims=True))
    high, mid, low = (part[:POS] for part in in_three(columns_to_rows(columns)))
    split = dim - queries
    low = jnp.concatenate([low[:, :split], low[:, split:]], axis=0)
    rest = jnp.concatenate([jnp.concatenate([high, mid], axis=0), low], axis=1).astype(BF16)
    for g in range(groups):
        note_ref[g, :plane, :] = raw_ref[...]
        note_ref[g, plane:, :] = rest


def score_call(shard, packet, raw, passages):
    rows, dim = passages.shape
    groups, plane, _ = packet.shape
    queries = groups * plane
    return pl.pallas_call(
        score_kernel,
        in_specs=[
            pl.BlockSpec(memory_space=pltpu.SMEM),
            pl.BlockSpec(memory_space=pltpu.VMEM),
            pl.BlockSpec(memory_space=pltpu.VMEM),
            pl.BlockSpec(memory_space=pltpu.HBM),
        ],
        out_shape=[
            jax.ShapeDtypeStruct((queries, rows), F32),
            jax.ShapeDtypeStruct((groups, plane + 8, dim), BF16),
            jax.ShapeDtypeStruct((POS, queries, LANES), jnp.int32),
        ],
        scratch_shapes=[
            pltpu.VMEM((POS, queries, LANES), jnp.int32),
            pltpu.VMEM((POS, queries, LANES), F32),
            pltpu.VMEM((rows, dim), BF16),
            pltpu.SemaphoreType.DMA((8,)),
        ],
        compiler_params=params(24),
        cost_estimate=pl.CostEstimate(
            flops=4 * queries * rows * dim, bytes_accessed=rows * dim * 2 + queries * rows * 4, transcendentals=0
        ),
        name="score",
    )(shard, packet, raw, passages)


def read_kernel(notes_ref, out_ref):
    n, queries = out_ref.shape[0], out_ref.shape[2]
    first = notes_ref.shape[1] - 8
    split = notes_ref.shape[2] - queries
    table = jnp.zeros((POS, queries), F32)
    for g in range(notes_ref.shape[0]):
        rest = notes_ref[g, first:, :].astype(F32)
        low = jnp.concatenate([rest[:POS, queries:], rest[POS:, queries:]], axis=1)
        table = table + ((rest[:POS, :queries] + rest[POS:, :queries]) + low)
    table = jnp.concatenate([table, jnp.zeros((8 - POS, queries), F32)], axis=0)
    for g in range(n):
        out_ref[g] = table


def read_call(notes, n, queries):
    return pl.pallas_call(
        read_kernel,
        out_shape=jax.ShapeDtypeStruct((n, 8, queries), F32),
        compiler_params=params(6),
        name="read",
    )(notes)


def sigmoid_kernel(scale, pos_ref, scores_ref, slopes_ref, sums_ref, pos, sums):
    queries, width = scores_ref.shape
    size = 16
    rows = pos_ref[0]
    for g in range(1, pos_ref.shape[0]):
        rows = rows + pos_ref[g]
    pos[...] = rows_to_columns(rows)

    def tile(t, carry):
        at = pl.ds(pl.multiple_of(t * size, size), size)
        columns = pos[at, :]
        p = [jnp.broadcast_to(columns[:, k : k + 1], (size, LANES)) for k in range(POS)]
        slope_acc = [jnp.zeros((size, LANES), F32) for _ in range(POS)]
        loss_acc = jnp.zeros((size, LANES), F32)
        for c in range(width // LANES):
            s = scores_ref[at, c * LANES : (c + 1) * LANES]
            sigs = [jax.nn.sigmoid(s - p[k]) for k in range(POS)]
            slopes = [sig * (1.0 - sig) for sig in sigs]
            loss_acc = loss_acc + ((sigs[0] + sigs[1]) + (sigs[2] + sigs[3]))
            slope_acc = [slope_acc[k] + slopes[k] for k in range(POS)]
            both = (slopes[0] + slopes[1]) + (slopes[2] + slopes[3])
            slopes_ref[at, c * LANES : (c + 1) * LANES] = both * scale
        for k in range(POS):
            sums[k, at, :] = slope_acc[k]
        sums[POS, at, :] = loss_acc
        return carry

    lax.fori_loop(0, queries // size, tile, 0)
    columns = [jnp.sum(sums[k], axis=1, keepdims=True) * (scale if k == POS else -scale) for k in range(POS + 1)]
    rows = columns_to_rows(columns)
    for g in range(sums_ref.shape[0]):
        sums_ref[g] = rows


def sigmoid_call(pos, scores, scale, groups):
    queries, width = scores.shape
    return pl.pallas_call(
        functools.partial(sigmoid_kernel, scale),
        in_specs=[pl.BlockSpec(memory_space=pltpu.VMEM)] * 2,
        out_shape=[
            jax.ShapeDtypeStruct((queries, width), F32),
            jax.ShapeDtypeStruct((groups, 8, queries), F32),
        ],
        scratch_shapes=[
            pltpu.VMEM((queries, LANES), F32),
            pltpu.VMEM((POS + 1, queries, LANES), F32),
        ],
        compiler_params=params(24),
        cost_estimate=pl.CostEstimate(
            flops=40 * queries * width, bytes_accessed=queries * width * 8, transcendentals=8 * queries * width
        ),
        input_output_aliases={1: 0},
        name="sigmoid",
    )(pos, scores)


def grad_kernel(
    sums_ref, slopes_ref, passages_hbm, ids_ref, part_ref, total_ref, grads, left_a, left_b, acc, passages, sems
):
    queries, rows = slopes_ref.shape
    width = left_a.shape[1]
    steps = sems.shape[0]
    copy = passage_copies(passages_hbm, passages, sems)
    for j in range(steps):
        copy(j).start()
    table = sums_ref[0]
    for g in range(1, sums_ref.shape[0]):
        table = table + sums_ref[g]
    total_ref[...] = table
    columns = rows_to_columns(table)
    for k in range(POS):
        give = columns[:, k : k + 1]
        for other in range(POS):
            if other != k:
                same = ids_ref[k] == ids_ref[other]
                give = give + jnp.where(same, columns[:, other : other + 1], 0.0)
        grads[k] = jnp.broadcast_to(give, (queries, LANES))

    def build(left, j):
        lane = lax.broadcasted_iota(jnp.int32, (16, LANES), 1) + j * width
        for tile in range(queries // 16):
            here = slice(tile * 16, tile * 16 + 16)
            want = [ids_ref[k, here, :] - lane for k in range(POS)]
            give = [grads[k, here, :] for k in range(POS)]
            for c in range(width // LANES):
                extra = jnp.zeros((16, LANES), F32)
                for k in range(POS):
                    extra = jnp.where(want[k] == c * LANES, give[k], extra)
                at = pl.ds(pl.multiple_of(j * width + c * LANES, LANES), LANES)
                left[here, c * LANES : (c + 1) * LANES] = (slopes_ref[here, at] + extra).astype(BF16)

    def product(left, j):
        copy(j).wait()
        block = passages[pl.ds(pl.multiple_of(j * width, width), width), :]
        return jnp.dot(left[...], block, preferred_element_type=F32)

    build(left_a, 0)
    for j in range(steps):
        now, later = (left_a, left_b) if j % 2 == 0 else (left_b, left_a)
        if j + 1 < steps:
            build(later, j + 1)
        term = product(now, j)
        if j == 0:
            acc[...] = term
        elif j + 1 < steps:
            acc[...] += term
        else:
            part_ref[...] = (acc[...] + term).astype(BF16).reshape(part_ref.shape)


def grad_call(sums, slopes, passages, ids, groups, block=1024):
    rows, dim = passages.shape
    queries = slopes.shape[0]
    return pl.pallas_call(
        grad_kernel,
        in_specs=[
            pl.BlockSpec(memory_space=pltpu.VMEM),
            pl.BlockSpec(memory_space=pltpu.VMEM),
            pl.BlockSpec(memory_space=pltpu.HBM),
            pl.BlockSpec(memory_space=pltpu.VMEM),
        ],
        out_shape=[
            jax.ShapeDtypeStruct((groups, queries // groups, dim), BF16),
            jax.ShapeDtypeStruct((8, queries), F32),
        ],
        scratch_shapes=[
            pltpu.VMEM((POS, queries, LANES), F32),
            pltpu.VMEM((queries, block), BF16),
            pltpu.VMEM((queries, block), BF16),
            pltpu.VMEM((queries, dim), F32),
            pltpu.VMEM((rows, dim), BF16),
            pltpu.SemaphoreType.DMA((rows // block,)),
        ],
        compiler_params=params(30),
        cost_estimate=pl.CostEstimate(
            flops=4 * queries * rows * dim, bytes_accessed=rows * dim * 2 + queries * rows * 4, transcendentals=0
        ),
        name="grad",
    )(sums, slopes, passages, ids)


def fold_kernel(parts_ref, out_ref):
    acc = parts_ref[0].astype(F32)
    for g in range(1, parts_ref.shape[0]):
        acc = acc + parts_ref[g].astype(F32)
    for g in range(out_ref.shape[0]):
        out_ref[g] = acc.astype(out_ref.dtype)


def fold_call(parts, n):
    return pl.pallas_call(
        fold_kernel,
        out_shape=jax.ShapeDtypeStruct((n,) + parts.shape[1:], parts.dtype),
        compiler_params=params(6),
        name="fold",
    )(parts)


def fold_both_kernel(parts_ref, out_ref, sum_ref):
    acc = parts_ref[0].astype(F32)
    for g in range(1, parts_ref.shape[0]):
        acc = acc + parts_ref[g].astype(F32)
    sum_ref[...] = acc
    for g in range(out_ref.shape[0]):
        out_ref[g] = acc.astype(out_ref.dtype)


def fold_both_call(parts, n):
    return pl.pallas_call(
        fold_both_kernel,
        out_shape=[
            jax.ShapeDtypeStruct((n,) + parts.shape[1:], parts.dtype),
            jax.ShapeDtypeStruct(parts.shape[1:], F32),
        ],
        compiler_params=params(6),
        name="fold_both",
    )(parts)


def final_kernel(core_ref, notes_ref, peer_ref, mine_ref, other_ref, out_ref):
    groups, plane, dim = mine_ref.shape
    queries = groups * plane

    def term(raw, grads):
        return lax.dot_general(raw, grads, (((0,), (0,)), ((), ())), preferred_element_type=F32)

    def both(first, second):
        out_ref[...] = term(*first)
        out_ref[...] += term(*second)

    own = (notes_ref[:, :plane, :].reshape(queries, dim), mine_ref[...].reshape(queries, dim))
    peer = (peer_ref[:, :plane, :].reshape(queries, dim), other_ref[...].reshape(queries, dim))

    @pl.when(core_ref[0] == 0)
    def _():
        both(own, peer)

    @pl.when(core_ref[0] != 0)
    def _():
        both(peer, own)


def final_call(core, notes, peer, mine, other):
    dim = mine.shape[-1]
    return pl.pallas_call(
        final_kernel,
        in_specs=[pl.BlockSpec(memory_space=pltpu.SMEM)] + [pl.BlockSpec(memory_space=pltpu.VMEM)] * 4,
        out_shape=jax.ShapeDtypeStruct((dim, dim), F32),
        compiler_params=params(20),
        name="final",
    )(core, notes, peer, mine, other)


def exchange(v, axes):
    return lax.all_to_all(v, axes, 0, 0, tiled=False)


def spread(v, axes):
    return exchange(jnp.broadcast_to(v[None], (lax.axis_size(axes),) + v.shape), axes)


def shards(queries_raw, projection, passages, positives):
    hp = lax.Precision.HIGHEST
    rows, dim = passages.shape
    own = queries_raw.shape[0]
    nz, nxy = lax.axis_size("z"), lax.axis_size(XY)
    plane = nz * own
    scale = 1.0 / (4.0 * rows * nz * nxy)
    core = lax.axis_index("c")
    swap = [(0, 1), (1, 0)]

    projected = jnp.dot(queries_raw, projection, precision=hp, preferred_element_type=F32)
    ids = jnp.concatenate([positives >> 14, (positives >> 7) & 127, positives & 127], axis=1)
    ids = jnp.pad(ids, ((0, 0), (0, LANES - 3 * POS)))
    packet = jnp.concatenate([projected.astype(BF16), ids.astype(BF16), queries_raw.astype(BF16)], axis=1)
    shard = (lax.axis_index("x") * nz + lax.axis_index("z")) * lax.axis_size("y") + lax.axis_index("y")
    packet, shard = lax.optimization_barrier((packet, shard))
    packet = spread(packet, "z").reshape(plane, 2 * dim + LANES)
    packet, raw = lax.optimization_barrier((packet[:, : dim + LANES], packet[:, dim + LANES :]))
    packet = spread(packet, XY)

    passages = pltpu.with_memory_space_constraint(passages, pltpu.HBM)
    scores, notes, local_pos = score_call(shard.reshape(1), packet, raw, passages)
    notes = exchange(notes, XY)
    peer = lax.ppermute(notes, "c", swap)
    pos = exchange(read_call(notes, nz, nxy * plane), "z")
    pos, peer = lax.optimization_barrier((pos, peer))
    slopes, sums = sigmoid_call(pos, scores, scale, nxy)
    sums = exchange(fold_call(exchange(sums, XY), nz), "z")
    part, sums = grad_call(sums, slopes, passages, local_pos, nxy)

    part = exchange(fold_call(exchange(part, XY), nz), "z")
    part, summed = fold_both_call(part, nxy)
    mine = exchange(part, XY)
    other = lax.ppermute(mine, "c", swap)

    home = lax.axis_index("z") * own
    query_grad = lax.dynamic_slice_in_dim(summed, home, own, 0)
    grad_raw = jnp.dot(query_grad, projection.T, precision=hp, preferred_element_type=F32)
    first = lax.axis_index(XY) * plane + home
    loss = lax.dynamic_slice_in_dim(sums[POS], first, own, 0)
    grad_projection = final_call(core.reshape(1), notes, peer, mine, other)
    return (loss, grad_raw, grad_projection)


def solution(mesh):
    axes = Mesh(mesh.devices.reshape(4, 8, 4, 2), ALL)
    in_specs = (P(ALL, None), P(), P(("x", "z", "y"), None), P(ALL, None))
    out_specs = (P(ALL), P(ALL, None), P())
    return jax.shard_map(shards, mesh=axes, in_specs=in_specs, out_specs=out_specs, check_vma=False)
```

```python
import functools

import jax
import jax.numpy as jnp
from jax import lax
from jax.experimental import pallas as pl
from jax.experimental.pallas import tpu as pltpu
from jax.sharding import Mesh, PartitionSpec as P

POS = 4
ALL = ("x", "z", "y", "c")
XY = ("x", "y")
LANES = 128
BF16 = jnp.bfloat16
F32 = jnp.float32


def params(mib):
    return pltpu.CompilerParams(vmem_limit_bytes=mib * 1024 * 1024)


def passage_copies(far, near, sems):
    width = near.shape[0] // sems.shape[0]

    def copy(j):
        at = pl.ds(pl.multiple_of(j * width, width), width)
        return pltpu.make_async_copy(far.at[at, :], near.at[at, :], sems.at[j])

    return copy


def in_three(x):
    high = x.astype(BF16).astype(F32)
    rest = x - high
    mid = rest.astype(BF16).astype(F32)
    return high, mid, rest - mid


def columns_to_rows(columns):
    rows = columns[0].shape[0]
    lane = lax.broadcasted_iota(jnp.int32, (rows, LANES), 1)
    table = jnp.zeros((rows, LANES), F32)
    for k, column in enumerate(columns):
        table = jnp.where(lane == k, column, table)
    return table.T[:8]


def rows_to_columns(rows):
    wide = jnp.concatenate([rows, jnp.zeros((LANES - 8, rows.shape[1]), F32)], axis=0)
    return wide.T


def score_kernel(shard_ref, packet_ref, raw_ref, passages_hbm, scores_ref, note_ref, ids_ref, chunk, found, passages, sems):
    groups, plane, _ = packet_ref.shape
    rows, dim = passages.shape
    queries = groups * plane
    steps = sems.shape[0]
    width = rows // steps
    copy = passage_copies(passages_hbm, passages, sems)
    copy(0).start()

    codes = packet_ref[:, :, dim:].reshape(queries, LANES).astype(F32).astype(jnp.int32)
    for k in range(POS):
        high, mid, low = (codes[:, k + POS * part : k + POS * part + 1] for part in range(3))
        ids = (high << 14) + (mid << 7) + low - shard_ref[0] * rows
        ids = jnp.broadcast_to(ids, (queries, LANES))
        ids_ref[k] = ids
        chunk[k] = ids >> 7
    for j in range(1, 4):
        copy(j).start()
    found[...] = jnp.zeros_like(found)

    def product(j):
        at = pl.multiple_of(j * width, width)
        emb = packet_ref[:, :, :dim].reshape(queries, dim)
        scores_ref[:, pl.ds(at, width)] = lax.dot_general(
            emb, passages[pl.ds(at, width), :], (((1,), (1,)), ((), ())), preferred_element_type=F32
        )

    def extract(j):
        first = j * (width // LANES)
        for tile in range(queries // 8):
            here = slice(tile * 8, tile * 8 + 8)
            scores = [
                scores_ref[here, pl.ds(pl.multiple_of(j * width + c * LANES, LANES), LANES)]
                for c in range(width // LANES)
            ]
            for k in range(POS):
                want = chunk[k, here, :] - first
                best = found[k, here, :]
                for c, s in enumerate(scores):
                    best = jnp.where(want == c, s, best)
                found[k, here, :] = best

    def step(j, carry):
        @pl.when(j + 3 < steps)
        def _():
            copy(j + 3).start()

        copy(j).wait()
        extract(j - 1)
        product(j)
        return carry

    copy(0).wait()
    product(0)
    lax.fori_loop(1, steps, step, 0)
    extract(steps - 1)

    lane = lax.broadcasted_iota(jnp.int32, (queries, LANES), 1)
    columns = []
    for k in range(POS):
        hit = lane == (ids_ref[k] & (LANES - 1))
        columns.append(jnp.sum(jnp.where(hit, found[k], 0.0), axis=1, keepdims=True))
    high, mid, low = (part[:POS] for part in in_three(columns_to_rows(columns)))
    split = dim - queries
    low = jnp.concatenate([low[:, :split], low[:, split:]], axis=0)
    rest = jnp.concatenate([jnp.concatenate([high, mid], axis=0), low], axis=1).astype(BF16)
    for g in range(groups):
        note_ref[g, :plane, :] = raw_ref[...]
        note_ref[g, plane:, :] = rest


def score_call(shard, packet, raw, passages):
    rows, dim = passages.shape
    groups, plane, _ = packet.shape
    queries = groups * plane
    return pl.pallas_call(
        score_kernel,
        in_specs=[
            pl.BlockSpec(memory_space=pltpu.SMEM),
            pl.BlockSpec(memory_space=pltpu.VMEM),
            pl.BlockSpec(memory_space=pltpu.VMEM),
            pl.BlockSpec(memory_space=pltpu.HBM),
        ],
        out_shape=[
            jax.ShapeDtypeStruct((queries, rows), F32),
            jax.ShapeDtypeStruct((groups, plane + 8, dim), BF16),
            jax.ShapeDtypeStruct((POS, queries, LANES), jnp.int32),
        ],
        scratch_shapes=[
            pltpu.VMEM((POS, queries, LANES), jnp.int32),
            pltpu.VMEM((POS, queries, LANES), F32),
            pltpu.VMEM((rows, dim), BF16),
            pltpu.SemaphoreType.DMA((8,)),
        ],
        compiler_params=params(24),
        cost_estimate=pl.CostEstimate(
            flops=4 * queries * rows * dim, bytes_accessed=rows * dim * 2 + queries * rows * 4, transcendentals=0
        ),
        name="score",
    )(shard, packet, raw, passages)


def read_kernel(notes_ref, out_ref):
    n, queries = out_ref.shape[0], out_ref.shape[2]
    first = notes_ref.shape[1] - 8
    split = notes_ref.shape[2] - queries
    table = jnp.zeros((POS, queries), F32)
    for g in range(notes_ref.shape[0]):
        rest = notes_ref[g, first:, :].astype(F32)
        low = jnp.concatenate([rest[:POS, queries:], rest[POS:, queries:]], axis=1)
        table = table + ((rest[:POS, :queries] + rest[POS:, :queries]) + low)
    table = jnp.concatenate([table, jnp.zeros((8 - POS, queries), F32)], axis=0)
    for g in range(n):
        out_ref[g] = table


def read_call(notes, n, queries):
    return pl.pallas_call(
        read_kernel,
        out_shape=jax.ShapeDtypeStruct((n, 8, queries), F32),
        compiler_params=params(6),
        name="read",
    )(notes)


def sigmoid_kernel(scale, pos_ref, scores_ref, slopes_ref, sums_ref, pos, sums):
    queries, width = scores_ref.shape
    size = 16
    rows = pos_ref[0]
    for g in range(1, pos_ref.shape[0]):
        rows = rows + pos_ref[g]
    pos[...] = rows_to_columns(rows)

    def place(t):
        at = pl.ds(pl.multiple_of(t * size, size), size)
        columns = pos[at, :]
        return at, [jnp.broadcast_to(columns[:, k : k + 1], (size, LANES)) for k in range(POS)]

    def tile(t, carry):
        at, p = place(t)
        p = [0.5 * q for q in p]
        square_acc = [jnp.zeros((size, LANES), F32) for _ in range(POS)]
        tanh_acc = jnp.zeros((size, LANES), F32)
        for c in range(width // LANES):
            s = 0.5 * scores_ref[at, c * LANES : (c + 1) * LANES]
            tanhs = [jnp.tanh(s - p[k]) for k in range(POS)]
            squares = [th * th for th in tanhs]
            tanh_acc = tanh_acc + ((tanhs[0] + tanhs[1]) + (tanhs[2] + tanhs[3]))
            square_acc = [square_acc[k] + squares[k] for k in range(POS)]
            both = (squares[0] + squares[1]) + (squares[2] + squares[3])
            slopes_ref[at, c * LANES : (c + 1) * LANES] = float(POS) - both
        chunks = float(width // LANES)
        for k in range(POS):
            sums[k, at, :] = 0.25 * (chunks - square_acc[k])
        sums[POS, at, :] = 0.5 * (POS * chunks + tanh_acc)
        return carry

    lax.fori_loop(0, queries // size, tile, 0, unroll=2)

    def again(t):
        at, p = place(t)
        zero = jnp.zeros((size, LANES), F32)

        def chunk(c, acc):
            here = pl.ds(pl.multiple_of(c * LANES, LANES), LANES)
            s = scores_ref[at, here]
            acc, both = list(acc), zero
            for k in range(POS):
                x = s - p[k]
                e = jnp.exp(-jnp.abs(x))
                r = 1.0 / (1.0 + e)
                slope = e * r * r
                acc[k] = acc[k] + slope
                acc[POS] = acc[POS] + jnp.where(x < 0.0, e * r, r)
                both = both + slope
            slopes_ref[at, here] = 4.0 * both
            return tuple(acc)

        acc = lax.fori_loop(0, width // LANES, chunk, (zero,) * (POS + 1))
        for k in range(POS + 1):
            sums[k, at, :] = acc[k]

    def totals(at):
        return [jnp.sum(sums[k, at, :], axis=1, keepdims=True) for k in range(POS + 1)]

    def least(columns):
        return jnp.min((columns[0] + columns[1]) + (columns[2] + columns[3]))

    def finish(columns):
        rows = columns_to_rows([c * (scale if k == POS else -scale) for k, c in enumerate(columns)])
        for g in range(sums_ref.shape[0]):
            sums_ref[g] = rows

    columns = totals(slice(None))
    finish(columns)
    enough = width / 1024.0

    @pl.when(least(columns) < enough)
    def _():
        def check(t, carry):
            @pl.when(least(totals(place(t)[0])) < enough)
            def _():
                again(t)

            return carry

        lax.fori_loop(0, queries // size, check, 0)
        finish(totals(slice(None)))


def sigmoid_call(pos, scores, scale, groups):
    queries, width = scores.shape
    return pl.pallas_call(
        functools.partial(sigmoid_kernel, scale),
        in_specs=[pl.BlockSpec(memory_space=pltpu.VMEM)] * 2,
        out_shape=[
            jax.ShapeDtypeStruct((queries, width), F32),
            jax.ShapeDtypeStruct((groups, 8, queries), F32),
        ],
        scratch_shapes=[
            pltpu.VMEM((queries, LANES), F32),
            pltpu.VMEM((POS + 1, queries, LANES), F32),
        ],
        compiler_params=params(24),
        cost_estimate=pl.CostEstimate(
            flops=40 * queries * width, bytes_accessed=queries * width * 8, transcendentals=8 * queries * width
        ),
        name="sigmoid",
    )(pos, scores)


def grad_kernel(
    scale, sums_ref, slopes_ref, passages_hbm, ids_ref, part_ref, total_ref, grads, left_a, left_b, acc, passages, sems
):
    queries, rows = slopes_ref.shape
    width = left_a.shape[1]
    steps = sems.shape[0]
    copy = passage_copies(passages_hbm, passages, sems)
    copy(0).start()
    copy(1).start()
    table = sums_ref[0]
    for g in range(1, sums_ref.shape[0]):
        table = table + sums_ref[g]
    total_ref[...] = table
    columns = rows_to_columns(table) * (4.0 / scale)
    for k in range(POS):
        give = columns[:, k : k + 1]
        for other in range(POS):
            if other != k:
                same = ids_ref[k] == ids_ref[other]
                give = give + jnp.where(same, columns[:, other : other + 1], 0.0)
        grads[k] = jnp.broadcast_to(give, (queries, LANES))

    def build(left, j):
        lane = lax.broadcasted_iota(jnp.int32, (16, LANES), 1) + j * width
        for tile in range(queries // 16):
            here = slice(tile * 16, tile * 16 + 16)
            want = [ids_ref[k, here, :] - lane for k in range(POS)]
            give = [grads[k, here, :] for k in range(POS)]
            for c in range(width // LANES):
                extra = jnp.zeros((16, LANES), F32)
                for k in range(POS):
                    extra = jnp.where(want[k] == c * LANES, give[k], extra)
                at = pl.ds(pl.multiple_of(j * width + c * LANES, LANES), LANES)
                left[here, c * LANES : (c + 1) * LANES] = (slopes_ref[here, at] + extra).astype(BF16)

    def product(left, j):
        copy(j).wait()
        block = passages[pl.ds(pl.multiple_of(j * width, width), width), :]
        return jnp.dot(left[...], block, preferred_element_type=F32)

    build(left_a, 0)
    for j in range(steps):
        now, later = (left_a, left_b) if j % 2 == 0 else (left_b, left_a)
        if j + 2 < steps:
            copy(j + 2).start()
        if j + 1 < steps:
            build(later, j + 1)
        term = product(now, j)
        if j == 0:
            acc[...] = term
        elif j + 1 < steps:
            acc[...] += term
        else:
            part_ref[...] = ((acc[...] + term) * (0.25 * scale)).astype(BF16).reshape(part_ref.shape)


def grad_call(sums, slopes, passages, ids, scale, groups, block=1024):
    rows, dim = passages.shape
    queries = slopes.shape[0]
    return pl.pallas_call(
        functools.partial(grad_kernel, scale),
        in_specs=[
            pl.BlockSpec(memory_space=pltpu.VMEM),
            pl.BlockSpec(memory_space=pltpu.VMEM),
            pl.BlockSpec(memory_space=pltpu.HBM),
            pl.BlockSpec(memory_space=pltpu.VMEM),
        ],
        out_shape=[
            jax.ShapeDtypeStruct((groups, queries // groups, dim), BF16),
            jax.ShapeDtypeStruct((8, queries), F32),
        ],
        scratch_shapes=[
            pltpu.VMEM((POS, queries, LANES), F32),
            pltpu.VMEM((queries, block), BF16),
            pltpu.VMEM((queries, block), BF16),
            pltpu.VMEM((queries, dim), F32),
            pltpu.VMEM((rows, dim), BF16),
            pltpu.SemaphoreType.DMA((rows // block,)),
        ],
        compiler_params=params(30),
        cost_estimate=pl.CostEstimate(
            flops=4 * queries * rows * dim, bytes_accessed=rows * dim * 2 + queries * rows * 4, transcendentals=0
        ),
        name="grad",
    )(sums, slopes, passages, ids)


def fold_kernel(parts_ref, out_ref):
    acc = parts_ref[0].astype(F32)
    for g in range(1, parts_ref.shape[0]):
        acc = acc + parts_ref[g].astype(F32)
    for g in range(out_ref.shape[0]):
        out_ref[g] = acc.astype(out_ref.dtype)


def fold_call(parts, n):
    return pl.pallas_call(
        fold_kernel,
        out_shape=jax.ShapeDtypeStruct((n,) + parts.shape[1:], parts.dtype),
        compiler_params=params(6),
        name="fold",
    )(parts)


def fold_both_kernel(parts_ref, out_ref, sum_ref):
    acc = parts_ref[0].astype(F32)
    for g in range(1, parts_ref.shape[0]):
        acc = acc + parts_ref[g].astype(F32)
    sum_ref[...] = acc
    for g in range(out_ref.shape[0]):
        out_ref[g] = acc.astype(out_ref.dtype)


def fold_both_call(parts, n):
    return pl.pallas_call(
        fold_both_kernel,
        out_shape=[
            jax.ShapeDtypeStruct((n,) + parts.shape[1:], parts.dtype),
            jax.ShapeDtypeStruct(parts.shape[1:], F32),
        ],
        compiler_params=params(6),
        name="fold_both",
    )(parts)


def final_kernel(core_ref, notes_ref, peer_ref, mine_ref, other_ref, out_hbm, near, sems):
    groups, plane, dim = mine_ref.shape
    queries = groups * plane
    parts = sems.shape[0]
    width = dim // parts
    even = core_ref[0] == 0

    def ordered(own, peer):
        own, peer = own.reshape(queries, own.shape[-1]), peer.reshape(queries, peer.shape[-1])
        return jnp.where(even, own, peer), jnp.where(even, peer, own)

    def term(raw, grads):
        return lax.dot_general(raw, grads, (((0,), (0,)), ((), ())), preferred_element_type=F32)

    def copy(i):
        at = pl.ds(i * width, width)
        return pltpu.make_async_copy(near.at[at, :], out_hbm.at[at, :], sems.at[i])

    grads = ordered(mine_ref[...], other_ref[...])
    for i in range(parts):
        at = slice(i * width, (i + 1) * width)
        raw = ordered(notes_ref[:, :plane, at], peer_ref[:, :plane, at])
        near[at, :] = term(raw[0], grads[0]) + term(raw[1], grads[1])
        copy(i).start()
    for i in range(parts):
        copy(i).wait()


def final_call(core, notes, peer, mine, other):
    dim = mine.shape[-1]
    return pl.pallas_call(
        final_kernel,
        in_specs=[pl.BlockSpec(memory_space=pltpu.SMEM)] + [pl.BlockSpec(memory_space=pltpu.VMEM)] * 4,
        out_specs=pl.BlockSpec(memory_space=pl.ANY),
        out_shape=jax.ShapeDtypeStruct((dim, dim), F32),
        scratch_shapes=[pltpu.VMEM((dim, dim), F32), pltpu.SemaphoreType.DMA((3,))],
        compiler_params=params(20),
        name="final",
    )(core, notes, peer, mine, other)


def head_kernel(raw_ref, projection_ref, positives_ref, out_ref):
    own, dim = raw_ref.shape
    raw = raw_ref[...]
    projected = jnp.dot(raw, projection_ref[...], precision=lax.Precision.HIGHEST, preferred_element_type=F32)
    lane = lax.broadcasted_iota(jnp.int32, (own, LANES), 1)
    codes = jnp.zeros((own, LANES), jnp.int32)
    for k in range(POS):
        ids = positives_ref[:, k : k + 1]
        for part, piece in enumerate((ids >> 14, (ids >> 7) & 127, ids & 127)):
            codes = jnp.where(lane == k + POS * part, piece, codes)
    for g in range(out_ref.shape[0]):
        out_ref[g, :, :dim] = projected.astype(BF16)
        out_ref[g, :, dim : dim + LANES] = codes.astype(F32).astype(BF16)
        out_ref[g, :, dim + LANES :] = raw.astype(BF16)


def head_call(raw, projection, positives, n):
    own, dim = raw.shape
    return pl.pallas_call(
        head_kernel,
        out_shape=jax.ShapeDtypeStruct((n, own, 2 * dim + LANES), BF16),
        compiler_params=params(12),
        name="head",
    )(raw, projection, positives)


def exchange(v, axes):
    return lax.all_to_all(v, axes, 0, 0, tiled=False)


def spread(v, axes):
    return exchange(jnp.broadcast_to(v[None], (lax.axis_size(axes),) + v.shape), axes)


def shards(queries_raw, projection, passages, positives):
    hp = lax.Precision.HIGHEST
    rows, dim = passages.shape
    own = queries_raw.shape[0]
    nz, nxy = lax.axis_size("z"), lax.axis_size(XY)
    plane = nz * own
    scale = 1.0 / (4.0 * rows * nz * nxy)
    core = lax.axis_index("c")
    swap = [(0, 1), (1, 0)]

    shard = (lax.axis_index("x") * nz + lax.axis_index("z")) * lax.axis_size("y") + lax.axis_index("y")
    packet, shard = lax.optimization_barrier((head_call(queries_raw, projection, positives, nz), shard))
    packet = exchange(packet, "z").reshape(plane, 2 * dim + LANES)
    packet, raw = lax.optimization_barrier((packet[:, : dim + LANES], packet[:, dim + LANES :]))
    packet = spread(packet, XY)

    passages = pltpu.with_memory_space_constraint(passages, pltpu.HBM)
    scores, notes, local_pos = score_call(shard.reshape(1), packet, raw, passages)
    notes = exchange(notes, XY)
    pos = exchange(read_call(notes, nz, nxy * plane), "z")
    slopes, sums = sigmoid_call(pos, scores, scale, nxy)
    sums = exchange(fold_call(exchange(sums, XY), nz), "z")
    part, sums = grad_call(sums, slopes, passages, local_pos, scale, nxy)

    part, notes = lax.optimization_barrier((part, notes))
    peer = lax.ppermute(notes, "c", swap)
    part, peer = lax.optimization_barrier((exchange(part, XY), peer))
    part = exchange(fold_call(part, nz), "z")
    part, summed = fold_both_call(part, nxy)
    mine = exchange(part, XY)
    other = lax.ppermute(mine, "c", swap)

    home = lax.axis_index("z") * own
    query_grad = lax.dynamic_slice_in_dim(summed, home, own, 0)
    grad_raw = jnp.dot(query_grad, projection.T, precision=hp, preferred_element_type=F32)
    first = lax.axis_index(XY) * plane + home
    loss = lax.dynamic_slice_in_dim(sums[POS], first, own, 0)
    grad_projection = final_call(core.reshape(1), notes, peer, mine, other)
    return (loss, grad_raw, grad_projection)


def solution(mesh):
    axes = Mesh(mesh.devices.reshape(4, 8, 4, 2), ALL)
    in_specs = (P(ALL, None), P(), P(("x", "z", "y"), None), P(ALL, None))
    out_specs = (P(ALL), P(ALL, None), P())
    return jax.shard_map(shards, mesh=axes, in_specs=in_specs, out_specs=out_specs, check_vma=False)
```

```python
import functools

import jax
import jax.numpy as jnp
from jax import lax
from jax.experimental import pallas as pl
from jax.experimental.pallas import tpu as pltpu
from jax.sharding import Mesh, PartitionSpec as P

POS = 4
ALL = ("x", "z", "y", "c")
XY = ("x", "y")
LANES = 128
BF16 = jnp.bfloat16
F32 = jnp.float32


def params(mib):
    return pltpu.CompilerParams(vmem_limit_bytes=mib * 1024 * 1024)


def passage_copies(far, near, sems):
    width = near.shape[0] // sems.shape[0]

    def copy(j):
        at = pl.ds(pl.multiple_of(j * width, width), width)
        return pltpu.make_async_copy(far.at[at, :], near.at[at, :], sems.at[j])

    return copy


def in_three(x):
    high = x.astype(BF16).astype(F32)
    rest = x - high
    mid = rest.astype(BF16).astype(F32)
    return high, mid, rest - mid


def columns_to_rows(columns):
    rows = columns[0].shape[0]
    lane = lax.broadcasted_iota(jnp.int32, (rows, LANES), 1)
    table = jnp.zeros((rows, LANES), F32)
    for k, column in enumerate(columns):
        table = jnp.where(lane == k, column, table)
    return table.T[:8]


def rows_to_columns(rows):
    wide = jnp.concatenate([rows, jnp.zeros((LANES - 8, rows.shape[1]), F32)], axis=0)
    return wide.T


def score_kernel(shard_ref, packet_ref, raw_ref, passages_hbm, scores_ref, note_ref, ids_ref, chunk, found, passages, sems):
    groups, plane, _ = packet_ref.shape
    rows, dim = passages.shape
    queries = groups * plane
    steps = sems.shape[0]
    width = rows // steps
    copy = passage_copies(passages_hbm, passages, sems)
    copy(0).start()

    codes = packet_ref[:, :, dim:].reshape(queries, LANES).astype(F32).astype(jnp.int32)
    for k in range(POS):
        high, mid, low = (codes[:, k + POS * part : k + POS * part + 1] for part in range(3))
        ids = (high << 14) + (mid << 7) + low - shard_ref[0] * rows
        ids = jnp.broadcast_to(ids, (queries, LANES))
        ids_ref[k] = ids
        chunk[k] = ids >> 7
    for j in range(1, 4):
        copy(j).start()
    found[...] = jnp.zeros_like(found)

    def product(j):
        at = pl.multiple_of(j * width, width)
        emb = packet_ref[:, :, :dim].reshape(queries, dim)
        scores_ref[:, pl.ds(at, width)] = lax.dot_general(
            emb, passages[pl.ds(at, width), :], (((1,), (1,)), ((), ())), preferred_element_type=F32
        )

    def extract(j):
        first = j * (width // LANES)
        for tile in range(queries // 8):
            here = slice(tile * 8, tile * 8 + 8)
            scores = [
                scores_ref[here, pl.ds(pl.multiple_of(j * width + c * LANES, LANES), LANES)]
                for c in range(width // LANES)
            ]
            for k in range(POS):
                want = chunk[k, here, :] - first
                best = found[k, here, :]
                for c, s in enumerate(scores):
                    best = jnp.where(want == c, s, best)
                found[k, here, :] = best

    def step(j, carry):
        @pl.when(j + 3 < steps)
        def _():
            copy(j + 3).start()

        copy(j).wait()
        extract(j - 1)
        product(j)
        return carry

    copy(0).wait()
    product(0)
    lax.fori_loop(1, steps, step, 0)
    extract(steps - 1)

    lane = lax.broadcasted_iota(jnp.int32, (queries, LANES), 1)
    columns = []
    for k in range(POS):
        hit = lane == (ids_ref[k] & (LANES - 1))
        columns.append(jnp.sum(jnp.where(hit, found[k], 0.0), axis=1, keepdims=True))
    high, mid, low = (part[:POS] for part in in_three(columns_to_rows(columns)))
    split = dim - queries
    low = jnp.concatenate([low[:, :split], low[:, split:]], axis=0)
    rest = jnp.concatenate([jnp.concatenate([high, mid], axis=0), low], axis=1).astype(BF16)
    for g in range(groups):
        note_ref[g, :plane, :] = raw_ref[...]
        note_ref[g, plane:, :] = rest


def score_call(shard, packet, raw, passages):
    rows, dim = passages.shape
    groups, plane, _ = packet.shape
    queries = groups * plane
    return pl.pallas_call(
        score_kernel,
        in_specs=[
            pl.BlockSpec(memory_space=pltpu.SMEM),
            pl.BlockSpec(memory_space=pltpu.VMEM),
            pl.BlockSpec(memory_space=pltpu.VMEM),
            pl.BlockSpec(memory_space=pltpu.HBM),
        ],
        out_shape=[
            jax.ShapeDtypeStruct((queries, rows), F32),
            jax.ShapeDtypeStruct((groups, plane + 8, dim), BF16),
            jax.ShapeDtypeStruct((POS, queries, LANES), jnp.int32),
        ],
        scratch_shapes=[
            pltpu.VMEM((POS, queries, LANES), jnp.int32),
            pltpu.VMEM((POS, queries, LANES), F32),
            pltpu.VMEM((rows, dim), BF16),
            pltpu.SemaphoreType.DMA((8,)),
        ],
        compiler_params=params(24),
        cost_estimate=pl.CostEstimate(
            flops=4 * queries * rows * dim, bytes_accessed=rows * dim * 2 + queries * rows * 4, transcendentals=0
        ),
        name="score",
    )(shard, packet, raw, passages)


def read_kernel(notes_ref, out_ref):
    n, queries = out_ref.shape[0], out_ref.shape[2]
    first = notes_ref.shape[1] - 8
    split = notes_ref.shape[2] - queries
    table = jnp.zeros((POS, queries), F32)
    for g in range(notes_ref.shape[0]):
        rest = notes_ref[g, first:, :].astype(F32)
        low = jnp.concatenate([rest[:POS, queries:], rest[POS:, queries:]], axis=1)
        table = table + ((rest[:POS, :queries] + rest[POS:, :queries]) + low)
    table = jnp.concatenate([table, jnp.zeros((8 - POS, queries), F32)], axis=0)
    for g in range(n):
        out_ref[g] = table


def read_call(notes, n, queries):
    return pl.pallas_call(
        read_kernel,
        out_shape=jax.ShapeDtypeStruct((n, 8, queries), F32),
        compiler_params=params(6),
        name="read",
    )(notes)


def sigmoid_kernel(scale, pos_ref, scores_ref, slopes_ref, sums_ref, pos, sums):
    queries, width = scores_ref.shape
    size = 16
    rows = pos_ref[0]
    for g in range(1, pos_ref.shape[0]):
        rows = rows + pos_ref[g]
    pos[...] = rows_to_columns(rows)

    def place(t):
        at = pl.ds(pl.multiple_of(t * size, size), size)
        columns = pos[at, :]
        return at, [jnp.broadcast_to(columns[:, k : k + 1], (size, LANES)) for k in range(POS)]

    def tile(t, carry):
        at, p = place(t)
        p = [0.5 * q for q in p]
        square_acc = [jnp.zeros((size, LANES), F32) for _ in range(POS)]
        tanh_acc = jnp.zeros((size, LANES), F32)
        for c in range(width // LANES):
            s = 0.5 * scores_ref[at, c * LANES : (c + 1) * LANES]
            tanhs = [jnp.tanh(s - p[k]) for k in range(POS)]
            squares = [th * th for th in tanhs]
            tanh_acc = tanh_acc + ((tanhs[0] + tanhs[1]) + (tanhs[2] + tanhs[3]))
            square_acc = [square_acc[k] + squares[k] for k in range(POS)]
            both = (squares[0] + squares[1]) + (squares[2] + squares[3])
            slopes_ref[at, c * LANES : (c + 1) * LANES] = float(POS) - both
        chunks = float(width // LANES)
        for k in range(POS):
            sums[k, at, :] = 0.25 * (chunks - square_acc[k])
        sums[POS, at, :] = 0.5 * (POS * chunks + tanh_acc)
        return carry

    lax.fori_loop(0, queries // size, tile, 0, unroll=2)

    def again(t):
        at, p = place(t)
        zero = jnp.zeros((size, LANES), F32)

        def chunk(c, acc):
            here = pl.ds(pl.multiple_of(c * LANES, LANES), LANES)
            s = scores_ref[at, here]
            acc, both = list(acc), zero
            for k in range(POS):
                x = s - p[k]
                e = jnp.exp(-jnp.abs(x))
                r = 1.0 / (1.0 + e)
                slope = e * r * r
                acc[k] = acc[k] + slope
                acc[POS] = acc[POS] + jnp.where(x < 0.0, e * r, r)
                both = both + slope
            slopes_ref[at, here] = 4.0 * both
            return tuple(acc)

        acc = lax.fori_loop(0, width // LANES, chunk, (zero,) * (POS + 1))
        for k in range(POS + 1):
            sums[k, at, :] = acc[k]

    def totals(at):
        return [jnp.sum(sums[k, at, :], axis=1, keepdims=True) for k in range(POS + 1)]

    def least(columns):
        return jnp.min((columns[0] + columns[1]) + (columns[2] + columns[3]))

    def finish(columns):
        rows = columns_to_rows([c * (scale if k == POS else -scale) for k, c in enumerate(columns)])
        for g in range(sums_ref.shape[0]):
            sums_ref[g] = rows

    columns = totals(slice(None))
    finish(columns)
    enough = width / 1024.0

    @pl.when(least(columns) < enough)
    def _():
        def check(t, carry):
            @pl.when(least(totals(place(t)[0])) < enough)
            def _():
                again(t)

            return carry

        lax.fori_loop(0, queries // size, check, 0)
        finish(totals(slice(None)))


def sigmoid_call(pos, scores, scale, groups):
    queries, width = scores.shape
    return pl.pallas_call(
        functools.partial(sigmoid_kernel, scale),
        in_specs=[pl.BlockSpec(memory_space=pltpu.VMEM)] * 2,
        out_shape=[
            jax.ShapeDtypeStruct((queries, width), F32),
            jax.ShapeDtypeStruct((groups, 8, queries), F32),
        ],
        scratch_shapes=[
            pltpu.VMEM((queries, LANES), F32),
            pltpu.VMEM((POS + 1, queries, LANES), F32),
        ],
        compiler_params=params(24),
        cost_estimate=pl.CostEstimate(
            flops=40 * queries * width, bytes_accessed=queries * width * 8, transcendentals=8 * queries * width
        ),
        name="sigmoid",
    )(pos, scores)


def grad_kernel(
    scale, sums_ref, slopes_ref, passages_ref, ids_ref, part_ref, total_ref, grads, left_a, left_b, acc
):
    queries, rows = slopes_ref.shape
    width = left_a.shape[1]
    steps = rows // width
    table = sums_ref[0]
    for g in range(1, sums_ref.shape[0]):
        table = table + sums_ref[g]
    total_ref[...] = table
    columns = rows_to_columns(table) * (4.0 / scale)
    for k in range(POS):
        give = columns[:, k : k + 1]
        for other in range(POS):
            if other != k:
                same = ids_ref[k] == ids_ref[other]
                give = give + jnp.where(same, columns[:, other : other + 1], 0.0)
        grads[k] = jnp.broadcast_to(give, (queries, LANES))

    def build(left, j):
        lane = lax.broadcasted_iota(jnp.int32, (16, LANES), 1) + j * width
        for tile in range(queries // 16):
            here = slice(tile * 16, tile * 16 + 16)
            want = [ids_ref[k, here, :] - lane for k in range(POS)]
            give = [grads[k, here, :] for k in range(POS)]
            for c in range(width // LANES):
                extra = jnp.zeros((16, LANES), F32)
                for k in range(POS):
                    extra = jnp.where(want[k] == c * LANES, give[k], extra)
                at = pl.ds(pl.multiple_of(j * width + c * LANES, LANES), LANES)
                left[here, c * LANES : (c + 1) * LANES] = (slopes_ref[here, at] + extra).astype(BF16)

    def product(left, j):
        block = passages_ref[pl.ds(pl.multiple_of(j * width, width), width), :]
        return jnp.dot(left[...], block, preferred_element_type=F32)

    build(left_a, 0)
    for j in range(steps):
        now, later = (left_a, left_b) if j % 2 == 0 else (left_b, left_a)
        if j + 1 < steps:
            build(later, j + 1)
        term = product(now, j)
        if j == 0:
            acc[...] = term
        elif j + 1 < steps:
            acc[...] += term
        else:
            part_ref[...] = ((acc[...] + term) * (0.25 * scale)).astype(BF16).reshape(part_ref.shape)


def grad_call(sums, slopes, passages, ids, scale, groups, block=1024):
    rows, dim = passages.shape
    queries = slopes.shape[0]
    return pl.pallas_call(
        functools.partial(grad_kernel, scale),
        in_specs=[
            pl.BlockSpec(memory_space=pltpu.VMEM),
            pl.BlockSpec(memory_space=pltpu.VMEM),
            pl.BlockSpec(memory_space=pltpu.VMEM),
            pl.BlockSpec(memory_space=pltpu.VMEM),
        ],
        out_shape=[
            jax.ShapeDtypeStruct((groups, queries // groups, dim), BF16),
            jax.ShapeDtypeStruct((8, queries), F32),
        ],
        scratch_shapes=[
            pltpu.VMEM((POS, queries, LANES), F32),
            pltpu.VMEM((queries, block), BF16),
            pltpu.VMEM((queries, block), BF16),
            pltpu.VMEM((queries, dim), F32),
        ],
        compiler_params=params(30),
        cost_estimate=pl.CostEstimate(
            flops=4 * queries * rows * dim, bytes_accessed=rows * dim * 2 + queries * rows * 4, transcendentals=0
        ),
        name="grad",
    )(sums, slopes, passages, ids)


def fold_kernel(parts_ref, out_ref):
    acc = parts_ref[0].astype(F32)
    for g in range(1, parts_ref.shape[0]):
        acc = acc + parts_ref[g].astype(F32)
    for g in range(out_ref.shape[0]):
        out_ref[g] = acc.astype(out_ref.dtype)


def fold_call(parts, n):
    return pl.pallas_call(
        fold_kernel,
        out_shape=jax.ShapeDtypeStruct((n,) + parts.shape[1:], parts.dtype),
        compiler_params=params(6),
        name="fold",
    )(parts)


def fold_both_kernel(parts_ref, out_ref, sum_ref):
    acc = parts_ref[0].astype(F32)
    for g in range(1, parts_ref.shape[0]):
        acc = acc + parts_ref[g].astype(F32)
    sum_ref[...] = acc
    for g in range(out_ref.shape[0]):
        out_ref[g] = acc.astype(out_ref.dtype)


def fold_both_call(parts, n):
    return pl.pallas_call(
        fold_both_kernel,
        out_shape=[
            jax.ShapeDtypeStruct((n,) + parts.shape[1:], parts.dtype),
            jax.ShapeDtypeStruct(parts.shape[1:], F32),
        ],
        compiler_params=params(6),
        name="fold_both",
    )(parts)


def term_kernel(first, notes_ref, mine_ref, out_ref):
    groups, plane, dim = mine_ref.shape
    raw = notes_ref[:, :plane, first : first + out_ref.shape[0]].reshape(groups * plane, out_ref.shape[0])
    grads = mine_ref[...].reshape(groups * plane, dim)
    out_ref[...] = lax.dot_general(raw, grads, (((0,), (0,)), ((), ())), preferred_element_type=F32)


def term_call(notes, mine, first, width):
    dim = mine.shape[-1]
    return pl.pallas_call(
        functools.partial(term_kernel, first),
        out_shape=jax.ShapeDtypeStruct((width, dim), F32),
        compiler_params=params(12),
        cost_estimate=pl.CostEstimate(
            flops=4 * width * dim * mine.shape[0] * mine.shape[1], bytes_accessed=width * dim * 4, transcendentals=0
        ),
        name="term",
    )(notes, mine)


def join_kernel(first_ref, first_other_ref, second_ref, second_other_ref, out_ref):
    half = first_ref.shape[0]
    out_ref[:half, :] = first_ref[...] + first_other_ref[...]
    out_ref[half:, :] = second_ref[...] + second_other_ref[...]


def join_call(terms, others):
    half, dim = terms[0].shape
    return pl.pallas_call(
        join_kernel,
        out_shape=jax.ShapeDtypeStruct((2 * half, dim), F32),
        compiler_params=params(12),
        name="join",
    )(terms[0], others[0], terms[1], others[1])


def head_kernel(raw_hbm, projection_hbm, positives_hbm, out_ref, raw_ref, projection_ref, positives_ref, sems):
    far_near = ((projection_hbm, projection_ref), (raw_hbm, raw_ref), (positives_hbm, positives_ref))
    copies = [pltpu.make_async_copy(far, near, sems.at[i]) for i, (far, near) in enumerate(far_near)]
    for copy in copies:
        copy.start()
    own, dim = raw_ref.shape
    copies[2].wait()
    lane = lax.broadcasted_iota(jnp.int32, (own, LANES), 1)
    codes = jnp.zeros((own, LANES), jnp.int32)
    for k in range(POS):
        ids = positives_ref[:, k : k + 1]
        for part, piece in enumerate((ids >> 14, (ids >> 7) & 127, ids & 127)):
            codes = jnp.where(lane == k + POS * part, piece, codes)
    copies[1].wait()
    raw = raw_ref[...]
    for g in range(out_ref.shape[0]):
        out_ref[g, :, dim : dim + LANES] = codes.astype(F32).astype(BF16)
        out_ref[g, :, dim + LANES :] = raw.astype(BF16)
    copies[0].wait()
    projected = jnp.dot(raw, projection_ref[...], precision=lax.Precision.HIGHEST, preferred_element_type=F32)
    for g in range(out_ref.shape[0]):
        out_ref[g, :, :dim] = projected.astype(BF16)


def head_call(raw, projection, positives, n):
    own, dim = raw.shape
    arrays = (raw, projection, positives)
    return pl.pallas_call(
        head_kernel,
        in_specs=[pl.BlockSpec(memory_space=pltpu.HBM)] * 3,
        out_shape=jax.ShapeDtypeStruct((n, own, 2 * dim + LANES), BF16),
        scratch_shapes=[pltpu.VMEM(v.shape, v.dtype) for v in arrays] + [pltpu.SemaphoreType.DMA((3,))],
        compiler_params=params(12),
        name="head",
    )(*(pltpu.with_memory_space_constraint(v, pltpu.HBM) for v in arrays))


def exchange(v, axes):
    return lax.all_to_all(v, axes, 0, 0, tiled=False)


def spread(v, axes):
    return exchange(jnp.broadcast_to(v[None], (lax.axis_size(axes),) + v.shape), axes)


def shards(queries_raw, projection, passages, positives):
    hp = lax.Precision.HIGHEST
    rows, dim = passages.shape
    own = queries_raw.shape[0]
    nz, nxy = lax.axis_size("z"), lax.axis_size(XY)
    plane = nz * own
    scale = 1.0 / (4.0 * rows * nz * nxy)

    shard = (lax.axis_index("x") * nz + lax.axis_index("z")) * lax.axis_size("y") + lax.axis_index("y")
    packet, shard = lax.optimization_barrier((head_call(queries_raw, projection, positives, nz), shard))
    packet = exchange(packet, "z").reshape(plane, 2 * dim + LANES)
    packet, raw = lax.optimization_barrier((packet[:, : dim + LANES], packet[:, dim + LANES :]))
    packet = spread(packet, XY)

    held = pltpu.with_memory_space_constraint(passages, pltpu.HBM)
    scores, notes, local_pos = score_call(shard.reshape(1), packet, raw, held)
    notes = exchange(notes, XY)
    pos = exchange(read_call(notes, nz, nxy * plane), "z")
    slopes, sums = sigmoid_call(pos, scores, scale, nxy)
    sums = exchange(fold_call(exchange(sums, XY), nz), "z")
    part, sums = grad_call(sums, slopes, passages, local_pos, scale, nxy)

    part = exchange(fold_call(exchange(part, XY), nz), "z")
    part, summed = fold_both_call(part, nxy)
    mine = exchange(part, XY)
    half = dim // 2
    terms = [term_call(notes, mine, first, half) for first in (0, half)]
    others = [lax.ppermute(term, "c", [(0, 1), (1, 0)]) for term in terms]
    grad_projection = join_call(terms, others)

    home = lax.axis_index("z") * own
    query_grad = lax.dynamic_slice_in_dim(summed, home, own, 0)
    grad_raw = jnp.dot(query_grad, projection.T, precision=hp, preferred_element_type=F32)
    first = lax.axis_index(XY) * plane + home
    loss = lax.dynamic_slice_in_dim(sums[POS], first, own, 0)
    return (loss, grad_raw, grad_projection)


def solution(mesh):
    axes = Mesh(mesh.devices.reshape(4, 8, 4, 2), ALL)
    in_specs = (P(ALL, None), P(), P(("x", "z", "y"), None), P(ALL, None))
    out_specs = (P(ALL), P(ALL, None), P())
    return jax.shard_map(shards, mesh=axes, in_specs=in_specs, out_specs=out_specs, check_vma=False)
```

```python
import functools

import jax
import jax.numpy as jnp
from jax import lax
from jax.experimental import pallas as pl
from jax.experimental.pallas import tpu as pltpu
from jax.sharding import Mesh, PartitionSpec as P

POS = 4
ALL = ("x", "z", "y", "c")
XY = ("x", "y")
LANES = 128
BF16 = jnp.bfloat16
F32 = jnp.float32


def params(mib):
    return pltpu.CompilerParams(vmem_limit_bytes=mib * 1024 * 1024)


def passage_copies(far, near, sems):
    width = near.shape[0] // sems.shape[0]

    def copy(j):
        at = pl.ds(pl.multiple_of(j * width, width), width)
        return pltpu.make_async_copy(far.at[at, :], near.at[at, :], sems.at[j])

    return copy


def in_three(x):
    high = x.astype(BF16).astype(F32)
    rest = x - high
    mid = rest.astype(BF16).astype(F32)
    return high, mid, rest - mid


def columns_to_rows(columns):
    rows = columns[0].shape[0]
    lane = lax.broadcasted_iota(jnp.int32, (rows, LANES), 1)
    table = jnp.zeros((rows, LANES), F32)
    for k, column in enumerate(columns):
        table = jnp.where(lane == k, column, table)
    return table.T[:8]


def rows_to_columns(rows):
    wide = jnp.concatenate([rows, jnp.zeros((LANES - 8, rows.shape[1]), F32)], axis=0)
    return wide.T


def score_kernel(shard_ref, packet_ref, raw_ref, passages_hbm, scores_ref, note_ref, ids_ref, chunk, found, passages, sems):
    groups, plane, _ = packet_ref.shape
    rows, dim = passages.shape
    queries = groups * plane
    steps = sems.shape[0]
    width = rows // steps
    copy = passage_copies(passages_hbm, passages, sems)
    copy(0).start()

    codes = packet_ref[:, :, dim:].reshape(queries, LANES).astype(F32).astype(jnp.int32)
    for k in range(POS):
        high, mid, low = (codes[:, k + POS * part : k + POS * part + 1] for part in range(3))
        ids = (high << 14) + (mid << 7) + low - shard_ref[0] * rows
        ids = jnp.broadcast_to(ids, (queries, LANES))
        ids_ref[k] = ids
        chunk[k] = ids >> 7
    for j in range(1, 4):
        copy(j).start()
    found[...] = jnp.zeros_like(found)

    def product(j):
        at = pl.multiple_of(j * width, width)
        emb = packet_ref[:, :, :dim].reshape(queries, dim)
        scores_ref[:, pl.ds(at, width)] = lax.dot_general(
            emb, passages[pl.ds(at, width), :], (((1,), (1,)), ((), ())), preferred_element_type=F32
        )

    def extract(j):
        first = j * (width // LANES)
        for tile in range(queries // 8):
            here = slice(tile * 8, tile * 8 + 8)
            scores = [
                scores_ref[here, pl.ds(pl.multiple_of(j * width + c * LANES, LANES), LANES)]
                for c in range(width // LANES)
            ]
            for k in range(POS):
                want = chunk[k, here, :] - first
                best = found[k, here, :]
                for c, s in enumerate(scores):
                    best = jnp.where(want == c, s, best)
                found[k, here, :] = best

    def step(j, carry):
        @pl.when(j + 3 < steps)
        def _():
            copy(j + 3).start()

        copy(j).wait()
        extract(j - 1)
        product(j)
        return carry

    copy(0).wait()
    product(0)
    lax.fori_loop(1, steps, step, 0)
    extract(steps - 1)

    lane = lax.broadcasted_iota(jnp.int32, (queries, LANES), 1)
    columns = []
    for k in range(POS):
        hit = lane == (ids_ref[k] & (LANES - 1))
        columns.append(jnp.sum(jnp.where(hit, found[k], 0.0), axis=1, keepdims=True))
    high, mid, low = (part[:POS] for part in in_three(columns_to_rows(columns)))
    split = dim - queries
    low = jnp.concatenate([low[:, :split], low[:, split:]], axis=0)
    rest = jnp.concatenate([jnp.concatenate([high, mid], axis=0), low], axis=1).astype(BF16)
    for g in range(groups):
        note_ref[g, :plane, :] = raw_ref[...]
        note_ref[g, plane:, :] = rest


def score_call(shard, packet, raw, passages):
    rows, dim = passages.shape
    groups, plane, _ = packet.shape
    queries = groups * plane
    return pl.pallas_call(
        score_kernel,
        in_specs=[
            pl.BlockSpec(memory_space=pltpu.SMEM),
            pl.BlockSpec(memory_space=pltpu.VMEM),
            pl.BlockSpec(memory_space=pltpu.VMEM),
            pl.BlockSpec(memory_space=pltpu.HBM),
        ],
        out_shape=[
            jax.ShapeDtypeStruct((queries, rows), F32),
            jax.ShapeDtypeStruct((groups, plane + 8, dim), BF16),
            jax.ShapeDtypeStruct((POS, queries, LANES), jnp.int32),
        ],
        scratch_shapes=[
            pltpu.VMEM((POS, queries, LANES), jnp.int32),
            pltpu.VMEM((POS, queries, LANES), F32),
            pltpu.VMEM((rows, dim), BF16),
            pltpu.SemaphoreType.DMA((8,)),
        ],
        compiler_params=params(23),
        cost_estimate=pl.CostEstimate(
            flops=4 * queries * rows * dim, bytes_accessed=rows * dim * 2 + queries * rows * 4, transcendentals=0
        ),
        name="score",
    )(shard, packet, raw, passages)


def read_kernel(notes_ref, out_ref):
    n, queries = out_ref.shape[0], out_ref.shape[2]
    first = notes_ref.shape[1] - 8
    split = notes_ref.shape[2] - queries
    table = jnp.zeros((POS, queries), F32)
    for g in range(notes_ref.shape[0]):
        rest = notes_ref[g, first:, :].astype(F32)
        low = jnp.concatenate([rest[:POS, queries:], rest[POS:, queries:]], axis=1)
        table = table + ((rest[:POS, :queries] + rest[POS:, :queries]) + low)
    table = jnp.concatenate([table, jnp.zeros((8 - POS, queries), F32)], axis=0)
    for g in range(n):
        out_ref[g] = table


def read_call(notes, n, queries):
    return pl.pallas_call(
        read_kernel,
        out_shape=jax.ShapeDtypeStruct((n, 8, queries), F32),
        compiler_params=params(6),
        name="read",
    )(notes)


def sigmoid_kernel(scale, pos_ref, scores_ref, slopes_ref, sums_ref, pos, sums):
    queries, width = scores_ref.shape
    size = 16
    rows = pos_ref[0]
    for g in range(1, pos_ref.shape[0]):
        rows = rows + pos_ref[g]
    pos[...] = rows_to_columns(rows)

    def place(t):
        at = pl.ds(pl.multiple_of(t * size, size), size)
        columns = pos[at, :]
        return at, [jnp.broadcast_to(columns[:, k : k + 1], (size, LANES)) for k in range(POS)]

    def tile(t, carry):
        at, p = place(t)
        p = [0.5 * q for q in p]
        square_acc = [jnp.zeros((size, LANES), F32) for _ in range(POS)]
        tanh_acc = jnp.zeros((size, LANES), F32)
        for c in range(width // LANES):
            s = 0.5 * scores_ref[at, c * LANES : (c + 1) * LANES]
            tanhs = [jnp.tanh(s - p[k]) for k in range(POS)]
            squares = [th * th for th in tanhs]
            tanh_acc = tanh_acc + ((tanhs[0] + tanhs[1]) + (tanhs[2] + tanhs[3]))
            square_acc = [square_acc[k] + squares[k] for k in range(POS)]
            both = (squares[0] + squares[1]) + (squares[2] + squares[3])
            slopes_ref[at, c * LANES : (c + 1) * LANES] = float(POS) - both
        chunks = float(width // LANES)
        for k in range(POS):
            sums[k, at, :] = 0.25 * (chunks - square_acc[k])
        sums[POS, at, :] = 0.5 * (POS * chunks + tanh_acc)
        return carry

    lax.fori_loop(0, queries // size, tile, 0, unroll=4)

    def again(t):
        at, p = place(t)
        zero = jnp.zeros((size, LANES), F32)

        def chunk(c, acc):
            here = pl.ds(pl.multiple_of(c * LANES, LANES), LANES)
            s = scores_ref[at, here]
            acc, both = list(acc), zero
            for k in range(POS):
                x = s - p[k]
                e = jnp.exp(-jnp.abs(x))
                r = 1.0 / (1.0 + e)
                slope = e * r * r
                acc[k] = acc[k] + slope
                acc[POS] = acc[POS] + jnp.where(x < 0.0, e * r, r)
                both = both + slope
            slopes_ref[at, here] = 4.0 * both
            return tuple(acc)

        acc = lax.fori_loop(0, width // LANES, chunk, (zero,) * (POS + 1))
        for k in range(POS + 1):
            sums[k, at, :] = acc[k]

    def totals(at):
        return [jnp.sum(sums[k, at, :], axis=1, keepdims=True) for k in range(POS + 1)]

    def least(columns):
        return jnp.min((columns[0] + columns[1]) + (columns[2] + columns[3]))

    def finish(columns):
        rows = columns_to_rows([c * (scale if k == POS else -scale) for k, c in enumerate(columns)])
        for g in range(sums_ref.shape[0]):
            sums_ref[g] = rows

    columns = totals(slice(None))
    finish(columns)
    enough = width / 1024.0

    @pl.when(least(columns) < enough)
    def _():
        def check(t, carry):
            @pl.when(least(totals(place(t)[0])) < enough)
            def _():
                again(t)

            return carry

        lax.fori_loop(0, queries // size, check, 0)
        finish(totals(slice(None)))


def sigmoid_call(pos, scores, scale, groups):
    queries, width = scores.shape
    return pl.pallas_call(
        functools.partial(sigmoid_kernel, scale),
        in_specs=[pl.BlockSpec(memory_space=pltpu.VMEM)] * 2,
        out_shape=[
            jax.ShapeDtypeStruct((queries, width), F32),
            jax.ShapeDtypeStruct((groups, 8, queries), F32),
        ],
        scratch_shapes=[
            pltpu.VMEM((queries, LANES), F32),
            pltpu.VMEM((POS + 1, queries, LANES), F32),
        ],
        compiler_params=params(21),
        cost_estimate=pl.CostEstimate(
            flops=40 * queries * width, bytes_accessed=queries * width * 8, transcendentals=8 * queries * width
        ),
        name="sigmoid",
    )(pos, scores)


def grad_kernel(
    scale, sums_ref, slopes_ref, passages_ref, ids_ref, part_ref, total_ref, grads, left_a, left_b, acc
):
    queries, rows = slopes_ref.shape
    width = left_a.shape[1]
    steps = rows // width
    table = sums_ref[0]
    for g in range(1, sums_ref.shape[0]):
        table = table + sums_ref[g]
    total_ref[...] = table
    columns = rows_to_columns(table) * (4.0 / scale)
    for k in range(POS):
        give = columns[:, k : k + 1]
        for other in range(POS):
            if other != k:
                same = ids_ref[k] == ids_ref[other]
                give = give + jnp.where(same, columns[:, other : other + 1], 0.0)
        grads[k] = jnp.broadcast_to(give, (queries, LANES))

    def build(left, j):
        lane = lax.broadcasted_iota(jnp.int32, (16, LANES), 1) + j * width
        for tile in range(queries // 16):
            here = slice(tile * 16, tile * 16 + 16)
            want = [ids_ref[k, here, :] - lane for k in range(POS)]
            give = [grads[k, here, :] for k in range(POS)]
            for c in range(width // LANES):
                extra = jnp.zeros((16, LANES), F32)
                for k in range(POS):
                    extra = jnp.where(want[k] == c * LANES, give[k], extra)
                at = pl.ds(pl.multiple_of(j * width + c * LANES, LANES), LANES)
                left[here, c * LANES : (c + 1) * LANES] = (slopes_ref[here, at] + extra).astype(BF16)

    def product(left, j):
        block = passages_ref[pl.ds(pl.multiple_of(j * width, width), width), :]
        return jnp.dot(left[...], block, preferred_element_type=F32)

    build(left_a, 0)
    for j in range(steps):
        now, later = (left_a, left_b) if j % 2 == 0 else (left_b, left_a)
        if j + 1 < steps:
            build(later, j + 1)
        term = product(now, j)
        if j == 0:
            acc[...] = term
        elif j + 1 < steps:
            acc[...] += term
        else:
            part_ref[...] = ((acc[...] + term) * (0.25 * scale)).astype(BF16).reshape(part_ref.shape)


def grad_call(sums, slopes, passages, ids, scale, groups, block=1024):
    rows, dim = passages.shape
    queries = slopes.shape[0]
    return pl.pallas_call(
        functools.partial(grad_kernel, scale),
        in_specs=[
            pl.BlockSpec(memory_space=pltpu.VMEM),
            pl.BlockSpec(memory_space=pltpu.VMEM),
            pl.BlockSpec(memory_space=pltpu.VMEM),
            pl.BlockSpec(memory_space=pltpu.VMEM),
        ],
        out_shape=[
            jax.ShapeDtypeStruct((groups, queries // groups, dim), BF16),
            jax.ShapeDtypeStruct((8, queries), F32),
        ],
        scratch_shapes=[
            pltpu.VMEM((POS, queries, LANES), F32),
            pltpu.VMEM((queries, block), BF16),
            pltpu.VMEM((queries, block), BF16),
            pltpu.VMEM((queries, dim), F32),
        ],
        compiler_params=params(28),
        cost_estimate=pl.CostEstimate(
            flops=4 * queries * rows * dim, bytes_accessed=rows * dim * 2 + queries * rows * 4, transcendentals=0
        ),
        name="grad",
    )(sums, slopes, passages, ids)


def fold_kernel(parts_ref, out_ref):
    acc = parts_ref[0].astype(F32)
    for g in range(1, parts_ref.shape[0]):
        acc = acc + parts_ref[g].astype(F32)
    for g in range(out_ref.shape[0]):
        out_ref[g] = acc.astype(out_ref.dtype)


def fold_call(parts, n):
    return pl.pallas_call(
        fold_kernel,
        out_shape=jax.ShapeDtypeStruct((n,) + parts.shape[1:], parts.dtype),
        compiler_params=params(6),
        name="fold",
    )(parts)


def fold_both_kernel(parts_ref, out_ref, sum_ref):
    acc = parts_ref[0].astype(F32)
    for g in range(1, parts_ref.shape[0]):
        acc = acc + parts_ref[g].astype(F32)
    sum_ref[...] = acc
    for g in range(out_ref.shape[0]):
        out_ref[g] = acc.astype(out_ref.dtype)


def fold_both_call(parts, n):
    return pl.pallas_call(
        fold_both_kernel,
        out_shape=[
            jax.ShapeDtypeStruct((n,) + parts.shape[1:], parts.dtype),
            jax.ShapeDtypeStruct(parts.shape[1:], F32),
        ],
        compiler_params=params(6),
        name="fold_both",
    )(parts)


def term_kernel(first, notes_ref, mine_ref, out_ref):
    groups, plane, dim = mine_ref.shape
    raw = notes_ref[:, :plane, first : first + out_ref.shape[0]].reshape(groups * plane, out_ref.shape[0])
    grads = mine_ref[...].reshape(groups * plane, dim)
    out_ref[...] = lax.dot_general(raw, grads, (((0,), (0,)), ((), ())), preferred_element_type=F32)


def term_call(notes, mine, first, width):
    dim = mine.shape[-1]
    return pl.pallas_call(
        functools.partial(term_kernel, first),
        out_shape=jax.ShapeDtypeStruct((width, dim), F32),
        compiler_params=params(12),
        cost_estimate=pl.CostEstimate(
            flops=4 * width * dim * mine.shape[0] * mine.shape[1], bytes_accessed=width * dim * 4, transcendentals=0
        ),
        name="term",
    )(notes, mine)


def join_kernel(first_ref, first_other_ref, second_ref, second_other_ref, out_hbm, near, sems):
    half = first_ref.shape[0]
    parts = sems.shape[0] // 2
    width = half // parts
    copies = []
    for begin, own_ref, other_ref in ((0, first_ref, first_other_ref), (half, second_ref, second_other_ref)):
        for i in range(parts):
            here = slice(i * width, (i + 1) * width)
            at = pl.ds(begin + i * width, width)
            near[at, :] = own_ref[here, :] + other_ref[here, :]
            copies.append(pltpu.make_async_copy(near.at[at, :], out_hbm.at[at, :], sems.at[len(copies)]))
            copies[-1].start()
    for copy in copies:
        copy.wait()


def join_call(terms, others):
    half, dim = terms[0].shape
    return pl.pallas_call(
        join_kernel,
        out_specs=pl.BlockSpec(memory_space=pl.ANY),
        out_shape=jax.ShapeDtypeStruct((2 * half, dim), F32),
        scratch_shapes=[pltpu.VMEM((2 * half, dim), F32), pltpu.SemaphoreType.DMA((4,))],
        compiler_params=params(12),
        name="join",
    )(terms[0], others[0], terms[1], others[1])


def head_kernel(raw_hbm, projection_hbm, positives_hbm, out_ref, raw_ref, projection_ref, positives_ref, sems):
    far_near = ((projection_hbm, projection_ref), (raw_hbm, raw_ref), (positives_hbm, positives_ref))
    copies = [pltpu.make_async_copy(far, near, sems.at[i]) for i, (far, near) in enumerate(far_near)]
    for copy in copies:
        copy.start()
    own, dim = raw_ref.shape
    copies[2].wait()
    lane = lax.broadcasted_iota(jnp.int32, (own, LANES), 1)
    codes = jnp.zeros((own, LANES), jnp.int32)
    for k in range(POS):
        ids = positives_ref[:, k : k + 1]
        for part, piece in enumerate((ids >> 14, (ids >> 7) & 127, ids & 127)):
            codes = jnp.where(lane == k + POS * part, piece, codes)
    copies[1].wait()
    raw = raw_ref[...]
    for g in range(out_ref.shape[0]):
        out_ref[g, :, dim : dim + LANES] = codes.astype(F32).astype(BF16)
        out_ref[g, :, dim + LANES :] = raw.astype(BF16)
    copies[0].wait()
    projected = jnp.dot(raw, projection_ref[...], precision=lax.Precision.HIGHEST, preferred_element_type=F32)
    for g in range(out_ref.shape[0]):
        out_ref[g, :, :dim] = projected.astype(BF16)


def head_call(raw, projection, positives, n):
    own, dim = raw.shape
    arrays = (raw, projection, positives)
    return pl.pallas_call(
        head_kernel,
        in_specs=[pl.BlockSpec(memory_space=pltpu.HBM)] * 3,
        out_shape=jax.ShapeDtypeStruct((n, own, 2 * dim + LANES), BF16),
        scratch_shapes=[pltpu.VMEM(v.shape, v.dtype) for v in arrays] + [pltpu.SemaphoreType.DMA((3,))],
        compiler_params=params(12),
        name="head",
    )(*(pltpu.with_memory_space_constraint(v, pltpu.HBM) for v in arrays))


def exchange(v, axes):
    return lax.all_to_all(v, axes, 0, 0, tiled=False)


def spread(v, axes):
    return exchange(jnp.broadcast_to(v[None], (lax.axis_size(axes),) + v.shape), axes)


def shards(queries_raw, projection, passages, positives):
    rows, dim = passages.shape
    own = queries_raw.shape[0]
    nz, nxy = lax.axis_size("z"), lax.axis_size(XY)
    plane = nz * own
    scale = 1.0 / (4.0 * rows * nz * nxy)

    shard = (lax.axis_index("x") * nz + lax.axis_index("z")) * lax.axis_size("y") + lax.axis_index("y")
    packet, shard = lax.optimization_barrier((head_call(queries_raw, projection, positives, nz), shard))
    packet = exchange(packet, "z").reshape(plane, 2 * dim + LANES)
    packet, raw = lax.optimization_barrier((packet[:, : dim + LANES], packet[:, dim + LANES :]))
    packet = spread(packet, XY)

    held = pltpu.with_memory_space_constraint(passages, pltpu.HBM)
    scores, notes, local_pos = score_call(shard.reshape(1), packet, raw, held)
    notes = exchange(notes, XY)
    pos = exchange(read_call(notes, nz, nxy * plane), "z")
    slopes, sums = sigmoid_call(pos, scores, scale, nxy)
    sums = exchange(fold_call(exchange(sums, XY), nz), "z")
    part, sums = grad_call(sums, slopes, passages, local_pos, scale, nxy)

    part = exchange(fold_call(exchange(part, XY), nz), "z")
    part, summed = fold_both_call(part, nxy)
    mine = exchange(part, XY)
    half = dim // 2
    terms = [term_call(notes, mine, first, half) for first in (0, half)]
    others = [lax.ppermute(term, "c", [(0, 1), (1, 0)]) for term in terms]
    grad_projection = join_call(terms, others)

    query_grad = lax.dynamic_slice_in_dim(summed, lax.axis_index("z") * own, own, 0)
    grad_raw = jnp.dot(query_grad, projection.T, precision=lax.Precision.HIGHEST, preferred_element_type=F32)
    first = lax.axis_index(XY) * plane + lax.axis_index("z") * own
    loss = lax.dynamic_slice_in_dim(sums[POS], first, own, 0)
    return (loss, grad_raw, grad_projection)


def solution(mesh):
    axes = Mesh(mesh.devices.reshape(4, 8, 4, 2), ALL)
    in_specs = (P(ALL, None), P(), P(("x", "z", "y"), None), P(ALL, None))
    out_specs = (P(ALL), P(ALL, None), P())
    return jax.shard_map(shards, mesh=axes, in_specs=in_specs, out_specs=out_specs, check_vma=False)
```

```python
import functools

import jax
import jax.numpy as jnp
from jax import lax
from jax.experimental import pallas as pl
from jax.experimental.pallas import tpu as pltpu
from jax.sharding import Mesh, PartitionSpec as P

POS = 4
ALL = ("x", "z", "y", "c")
XY = ("x", "y")
LANES = 128
BF16 = jnp.bfloat16
F32 = jnp.float32


def params(mib):
    return pltpu.CompilerParams(vmem_limit_bytes=mib * 1024 * 1024)


def passage_copies(far, near, sems):
    width = near.shape[0] // sems.shape[0]

    def copy(j):
        at = pl.ds(pl.multiple_of(j * width, width), width)
        return pltpu.make_async_copy(far.at[at, :], near.at[at, :], sems.at[j])

    return copy


def in_three(x):
    high = x.astype(BF16).astype(F32)
    rest = x - high
    mid = rest.astype(BF16).astype(F32)
    return high, mid, rest - mid


def columns_to_rows(columns):
    rows = columns[0].shape[0]
    lane = lax.broadcasted_iota(jnp.int32, (rows, LANES), 1)
    table = jnp.zeros((rows, LANES), F32)
    for k, column in enumerate(columns):
        table = jnp.where(lane == k, column, table)
    return table.T[:8]


def rows_to_columns(rows):
    wide = jnp.concatenate([rows, jnp.zeros((LANES - 8, rows.shape[1]), F32)], axis=0)
    return wide.T


def score_kernel(shard_ref, packet_ref, raw_ref, passages_hbm, scores_ref, note_ref, ids_ref, chunk, found, passages, sems):
    groups, plane, _ = packet_ref.shape
    rows, dim = passages.shape
    queries = groups * plane
    steps = sems.shape[0]
    width = rows // steps
    copy = passage_copies(passages_hbm, passages, sems)
    copy(0).start()

    codes = packet_ref[:, :, dim:].reshape(queries, LANES).astype(F32).astype(jnp.int32)
    for k in range(POS):
        high, mid, low = (codes[:, k + POS * part : k + POS * part + 1] for part in range(3))
        ids = (high << 14) + (mid << 7) + low - shard_ref[0] * rows
        ids = jnp.broadcast_to(ids, (queries, LANES))
        ids_ref[k] = ids
        chunk[k] = ids >> 7
    for j in range(1, 4):
        copy(j).start()
    found[...] = jnp.zeros_like(found)

    def product(j):
        at = pl.multiple_of(j * width, width)
        emb = packet_ref[:, :, :dim].reshape(queries, dim)
        scores_ref[:, pl.ds(at, width)] = lax.dot_general(
            emb, passages[pl.ds(at, width), :], (((1,), (1,)), ((), ())), preferred_element_type=F32
        )

    def extract(j):
        first = j * (width // LANES)
        for tile in range(queries // 8):
            here = slice(tile * 8, tile * 8 + 8)
            scores = [
                scores_ref[here, pl.ds(pl.multiple_of(j * width + c * LANES, LANES), LANES)]
                for c in range(width // LANES)
            ]
            for k in range(POS):
                want = chunk[k, here, :] - first
                best = found[k, here, :]
                for c, s in enumerate(scores):
                    best = jnp.where(want == c, s, best)
                found[k, here, :] = best

    def step(j, carry):
        @pl.when(j + 3 < steps)
        def _():
            copy(j + 3).start()

        copy(j).wait()
        extract(j - 1)
        product(j)
        return carry

    copy(0).wait()
    product(0)
    lax.fori_loop(1, steps, step, 0)
    extract(steps - 1)

    lane = lax.broadcasted_iota(jnp.int32, (queries, LANES), 1)
    columns = []
    for k in range(POS):
        hit = lane == (ids_ref[k] & (LANES - 1))
        columns.append(jnp.sum(jnp.where(hit, found[k], 0.0), axis=1, keepdims=True))
    high, mid, low = (part[:POS] for part in in_three(columns_to_rows(columns)))
    split = dim - queries
    low = jnp.concatenate([low[:, :split], low[:, split:]], axis=0)
    rest = jnp.concatenate([jnp.concatenate([high, mid], axis=0), low], axis=1).astype(BF16)
    for g in range(groups):
        note_ref[g, :plane, :] = raw_ref[...]
        note_ref[g, plane:, :] = rest


def score_call(shard, packet, raw, passages):
    rows, dim = passages.shape
    groups, plane, _ = packet.shape
    queries = groups * plane
    return pl.pallas_call(
        score_kernel,
        in_specs=[
            pl.BlockSpec(memory_space=pltpu.SMEM),
            pl.BlockSpec(memory_space=pltpu.VMEM),
            pl.BlockSpec(memory_space=pltpu.VMEM),
            pl.BlockSpec(memory_space=pltpu.HBM),
        ],
        out_shape=[
            jax.ShapeDtypeStruct((queries, rows), F32),
            jax.ShapeDtypeStruct((groups, plane + 8, dim), BF16),
            jax.ShapeDtypeStruct((POS, queries, LANES), jnp.int32),
        ],
        scratch_shapes=[
            pltpu.VMEM((POS, queries, LANES), jnp.int32),
            pltpu.VMEM((POS, queries, LANES), F32),
            pltpu.VMEM((rows, dim), BF16),
            pltpu.SemaphoreType.DMA((8,)),
        ],
        compiler_params=params(23),
        cost_estimate=pl.CostEstimate(
            flops=4 * queries * rows * dim, bytes_accessed=rows * dim * 2 + queries * rows * 4, transcendentals=0
        ),
        name="score",
    )(shard, packet, raw, passages)


def read_kernel(notes_ref, out_ref):
    n, queries = out_ref.shape[0], out_ref.shape[2]
    first = notes_ref.shape[1] - 8
    split = notes_ref.shape[2] - queries
    table = jnp.zeros((POS, queries), F32)
    for g in range(notes_ref.shape[0]):
        rest = notes_ref[g, first:, :].astype(F32)
        low = jnp.concatenate([rest[:POS, queries:], rest[POS:, queries:]], axis=1)
        table = table + ((rest[:POS, :queries] + rest[POS:, :queries]) + low)
    table = jnp.concatenate([table, jnp.zeros((8 - POS, queries), F32)], axis=0)
    for g in range(n):
        out_ref[g] = table


def read_call(notes, n, queries):
    return pl.pallas_call(
        read_kernel,
        out_shape=jax.ShapeDtypeStruct((n, 8, queries), F32),
        compiler_params=params(6),
        name="read",
    )(notes)


def sigmoid_kernel(scale, pos_ref, scores_ref, slopes_ref, sums_ref, pos, sums):
    queries, width = scores_ref.shape
    size = 16
    rows = pos_ref[0]
    for g in range(1, pos_ref.shape[0]):
        rows = rows + pos_ref[g]
    pos[...] = rows_to_columns(rows)

    def place(t):
        at = pl.ds(pl.multiple_of(t * size, size), size)
        columns = pos[at, :]
        return at, [jnp.broadcast_to(columns[:, k : k + 1], (size, LANES)) for k in range(POS)]

    def tile(t, carry):
        at, p = place(t)
        p = [0.5 * q for q in p]
        square_acc = [jnp.zeros((size, LANES), F32) for _ in range(POS)]
        tanh_acc = jnp.zeros((size, LANES), F32)
        for c in range(width // LANES):
            s = 0.5 * scores_ref[at, c * LANES : (c + 1) * LANES]
            tanhs = [jnp.tanh(s - p[k]) for k in range(POS)]
            squares = [th * th for th in tanhs]
            tanh_acc = tanh_acc + ((tanhs[0] + tanhs[1]) + (tanhs[2] + tanhs[3]))
            square_acc = [square_acc[k] + squares[k] for k in range(POS)]
            both = (squares[0] + squares[1]) + (squares[2] + squares[3])
            slopes_ref[at, c * LANES : (c + 1) * LANES] = float(POS) - both
        chunks = float(width // LANES)
        for k in range(POS):
            sums[k, at, :] = 0.25 * (chunks - square_acc[k])
        sums[POS, at, :] = 0.5 * (POS * chunks + tanh_acc)
        return carry

    lax.fori_loop(0, queries // size, tile, 0, unroll=8)

    def again(t):
        at, p = place(t)
        zero = jnp.zeros((size, LANES), F32)

        def chunk(c, acc):
            here = pl.ds(pl.multiple_of(c * LANES, LANES), LANES)
            s = scores_ref[at, here]
            acc, both = list(acc), zero
            for k in range(POS):
                x = s - p[k]
                e = jnp.exp(-jnp.abs(x))
                r = 1.0 / (1.0 + e)
                slope = e * r * r
                acc[k] = acc[k] + slope
                acc[POS] = acc[POS] + jnp.where(x < 0.0, e * r, r)
                both = both + slope
            slopes_ref[at, here] = 4.0 * both
            return tuple(acc)

        acc = lax.fori_loop(0, width // LANES, chunk, (zero,) * (POS + 1))
        for k in range(POS + 1):
            sums[k, at, :] = acc[k]

    def totals(at):
        return [jnp.sum(sums[k, at, :], axis=1, keepdims=True) for k in range(POS + 1)]

    def least(columns):
        return jnp.min((columns[0] + columns[1]) + (columns[2] + columns[3]))

    def finish(columns):
        rows = columns_to_rows([c * (scale if k == POS else -scale) for k, c in enumerate(columns)])
        for g in range(sums_ref.shape[0]):
            sums_ref[g] = rows

    columns = totals(slice(None))
    finish(columns)
    enough = width / 1024.0

    @pl.when(least(columns) < enough)
    def _():
        def check(t, carry):
            @pl.when(least(totals(place(t)[0])) < enough)
            def _():
                again(t)

            return carry

        lax.fori_loop(0, queries // size, check, 0)
        finish(totals(slice(None)))


def sigmoid_call(pos, scores, scale, groups):
    queries, width = scores.shape
    return pl.pallas_call(
        functools.partial(sigmoid_kernel, scale),
        in_specs=[pl.BlockSpec(memory_space=pltpu.VMEM)] * 2,
        out_shape=[
            jax.ShapeDtypeStruct((queries, width), F32),
            jax.ShapeDtypeStruct((groups, 8, queries), F32),
        ],
        scratch_shapes=[
            pltpu.VMEM((queries, LANES), F32),
            pltpu.VMEM((POS + 1, queries, LANES), F32),
        ],
        compiler_params=params(21),
        cost_estimate=pl.CostEstimate(
            flops=40 * queries * width, bytes_accessed=queries * width * 8, transcendentals=8 * queries * width
        ),
        name="sigmoid",
    )(pos, scores)


def grad_kernel(
    scale, sums_ref, slopes_ref, passages_ref, ids_ref, part_ref, total_ref, grads, left_a, left_b, acc
):
    queries, rows = slopes_ref.shape
    width = left_a.shape[1]
    steps = rows // width
    table = sums_ref[0]
    for g in range(1, sums_ref.shape[0]):
        table = table + sums_ref[g]
    total_ref[...] = table
    columns = rows_to_columns(table) * (4.0 / scale)
    for k in range(POS):
        give = columns[:, k : k + 1]
        for other in range(POS):
            if other != k:
                same = ids_ref[k] == ids_ref[other]
                give = give + jnp.where(same, columns[:, other : other + 1], 0.0)
        grads[k] = jnp.broadcast_to(give, (queries, LANES))

    def build(left, j):
        lane = lax.broadcasted_iota(jnp.int32, (16, LANES), 1) + j * width
        for tile in range(queries // 16):
            here = slice(tile * 16, tile * 16 + 16)
            want = [ids_ref[k, here, :] - lane for k in range(POS)]
            give = [grads[k, here, :] for k in range(POS)]
            for c in range(width // LANES):
                extra = jnp.zeros((16, LANES), F32)
                for k in range(POS):
                    extra = jnp.where(want[k] == c * LANES, give[k], extra)
                at = pl.ds(pl.multiple_of(j * width + c * LANES, LANES), LANES)
                left[here, c * LANES : (c + 1) * LANES] = (slopes_ref[here, at] + extra).astype(BF16)

    def product(left, j):
        block = passages_ref[pl.ds(pl.multiple_of(j * width, width), width), :]
        return jnp.dot(left[...], block, preferred_element_type=F32)

    build(left_a, 0)
    for j in range(steps):
        now, later = (left_a, left_b) if j % 2 == 0 else (left_b, left_a)
        if j + 1 < steps:
            build(later, j + 1)
        term = product(now, j)
        if j == 0:
            acc[...] = term
        elif j + 1 < steps:
            acc[...] += term
        else:
            part_ref[...] = ((acc[...] + term) * (0.25 * scale)).astype(BF16).reshape(part_ref.shape)


def grad_call(sums, slopes, passages, ids, scale, groups, block=1024):
    rows, dim = passages.shape
    queries = slopes.shape[0]
    return pl.pallas_call(
        functools.partial(grad_kernel, scale),
        in_specs=[
            pl.BlockSpec(memory_space=pltpu.VMEM),
            pl.BlockSpec(memory_space=pltpu.VMEM),
            pl.BlockSpec(memory_space=pltpu.VMEM),
            pl.BlockSpec(memory_space=pltpu.VMEM),
        ],
        out_shape=[
            jax.ShapeDtypeStruct((groups, queries // groups, dim), BF16),
            jax.ShapeDtypeStruct((8, queries), F32),
        ],
        scratch_shapes=[
            pltpu.VMEM((POS, queries, LANES), F32),
            pltpu.VMEM((queries, block), BF16),
            pltpu.VMEM((queries, block), BF16),
            pltpu.VMEM((queries, dim), F32),
        ],
        compiler_params=params(28),
        cost_estimate=pl.CostEstimate(
            flops=4 * queries * rows * dim, bytes_accessed=rows * dim * 2 + queries * rows * 4, transcendentals=0
        ),
        name="grad",
    )(sums, slopes, passages, ids)


def fold_kernel(parts_ref, out_ref):
    acc = parts_ref[0].astype(F32)
    for g in range(1, parts_ref.shape[0]):
        acc = acc + parts_ref[g].astype(F32)
    for g in range(out_ref.shape[0]):
        out_ref[g] = acc.astype(out_ref.dtype)


def fold_call(parts, n):
    return pl.pallas_call(
        fold_kernel,
        out_shape=jax.ShapeDtypeStruct((n,) + parts.shape[1:], parts.dtype),
        compiler_params=params(6),
        name="fold",
    )(parts)


def fold_both_kernel(parts_ref, out_ref, sum_ref):
    acc = parts_ref[0].astype(F32)
    for g in range(1, parts_ref.shape[0]):
        acc = acc + parts_ref[g].astype(F32)
    sum_ref[...] = acc
    for g in range(out_ref.shape[0]):
        out_ref[g] = acc.astype(out_ref.dtype)


def fold_both_call(parts, n):
    return pl.pallas_call(
        fold_both_kernel,
        out_shape=[
            jax.ShapeDtypeStruct((n,) + parts.shape[1:], parts.dtype),
            jax.ShapeDtypeStruct(parts.shape[1:], F32),
        ],
        compiler_params=params(6),
        name="fold_both",
    )(parts)


def term_kernel(first, notes_ref, mine_ref, out_ref):
    groups, plane, dim = mine_ref.shape
    raw = notes_ref[:, :plane, first : first + out_ref.shape[0]].reshape(groups * plane, out_ref.shape[0])
    grads = mine_ref[...].reshape(groups * plane, dim)
    out_ref[...] = lax.dot_general(raw, grads, (((0,), (0,)), ((), ())), preferred_element_type=F32)


def term_call(notes, mine, first, width):
    dim = mine.shape[-1]
    return pl.pallas_call(
        functools.partial(term_kernel, first),
        out_shape=jax.ShapeDtypeStruct((width, dim), F32),
        compiler_params=params(12),
        cost_estimate=pl.CostEstimate(
            flops=4 * width * dim * mine.shape[0] * mine.shape[1], bytes_accessed=width * dim * 4, transcendentals=0
        ),
        name="term",
    )(notes, mine)


def join_kernel(first_ref, first_other_ref, second_ref, second_other_ref, out_hbm, near, sems):
    half = first_ref.shape[0]
    parts = sems.shape[0] // 2
    width = half // parts
    copies = []
    for begin, own_ref, other_ref in ((0, first_ref, first_other_ref), (half, second_ref, second_other_ref)):
        for i in range(parts):
            here = slice(i * width, (i + 1) * width)
            at = pl.ds(begin + i * width, width)
            near[at, :] = own_ref[here, :] + other_ref[here, :]
            copies.append(pltpu.make_async_copy(near.at[at, :], out_hbm.at[at, :], sems.at[len(copies)]))
            copies[-1].start()
    for copy in copies:
        copy.wait()


def join_call(terms, others):
    half, dim = terms[0].shape
    return pl.pallas_call(
        join_kernel,
        out_specs=pl.BlockSpec(memory_space=pl.ANY),
        out_shape=jax.ShapeDtypeStruct((2 * half, dim), F32),
        scratch_shapes=[pltpu.VMEM((2 * half, dim), F32), pltpu.SemaphoreType.DMA((4,))],
        compiler_params=params(12),
        name="join",
    )(terms[0], others[0], terms[1], others[1])


def head_kernel(raw_hbm, projection_hbm, positives_hbm, out_ref, raw_ref, projection_ref, positives_ref, sems):
    far_near = ((projection_hbm, projection_ref), (raw_hbm, raw_ref), (positives_hbm, positives_ref))
    copies = [pltpu.make_async_copy(far, near, sems.at[i]) for i, (far, near) in enumerate(far_near)]
    for copy in copies:
        copy.start()
    own, dim = raw_ref.shape
    copies[2].wait()
    lane = lax.broadcasted_iota(jnp.int32, (own, LANES), 1)
    codes = jnp.zeros((own, LANES), jnp.int32)
    for k in range(POS):
        ids = positives_ref[:, k : k + 1]
        for part, piece in enumerate((ids >> 14, (ids >> 7) & 127, ids & 127)):
            codes = jnp.where(lane == k + POS * part, piece, codes)
    copies[1].wait()
    raw = raw_ref[...]
    for g in range(out_ref.shape[0]):
        out_ref[g, :, dim : dim + LANES] = codes.astype(F32).astype(BF16)
        out_ref[g, :, dim + LANES :] = raw.astype(BF16)
    copies[0].wait()
    projected = jnp.dot(raw, projection_ref[...], precision=lax.Precision.HIGHEST, preferred_element_type=F32)
    for g in range(out_ref.shape[0]):
        out_ref[g, :, :dim] = projected.astype(BF16)


def head_call(raw, projection, positives, n):
    own, dim = raw.shape
    arrays = (raw, projection, positives)
    return pl.pallas_call(
        head_kernel,
        in_specs=[pl.BlockSpec(memory_space=pltpu.HBM)] * 3,
        out_shape=jax.ShapeDtypeStruct((n, own, 2 * dim + LANES), BF16),
        scratch_shapes=[pltpu.VMEM(v.shape, v.dtype) for v in arrays] + [pltpu.SemaphoreType.DMA((3,))],
        compiler_params=params(12),
        name="head",
    )(*(pltpu.with_memory_space_constraint(v, pltpu.HBM) for v in arrays))


def exchange(v, axes):
    return lax.all_to_all(v, axes, 0, 0, tiled=False)


def spread(v, axes):
    return exchange(jnp.broadcast_to(v[None], (lax.axis_size(axes),) + v.shape), axes)


def shards(queries_raw, projection, passages, positives):
    rows, dim = passages.shape
    own = queries_raw.shape[0]
    nz, nxy = lax.axis_size("z"), lax.axis_size(XY)
    plane = nz * own
    scale = 1.0 / (4.0 * rows * nz * nxy)

    shard = (lax.axis_index("x") * nz + lax.axis_index("z")) * lax.axis_size("y") + lax.axis_index("y")
    packet, shard = lax.optimization_barrier((head_call(queries_raw, projection, positives, nz), shard))
    packet = exchange(packet, "z").reshape(plane, 2 * dim + LANES)
    packet, raw = lax.optimization_barrier((packet[:, : dim + LANES], packet[:, dim + LANES :]))
    packet = spread(packet, XY)

    held = pltpu.with_memory_space_constraint(passages, pltpu.HBM)
    scores, notes, local_pos = score_call(shard.reshape(1), packet, raw, held)
    notes = exchange(notes, XY)
    pos = exchange(read_call(notes, nz, nxy * plane), "z")
    slopes, sums = sigmoid_call(pos, scores, scale, nxy)
    sums = exchange(fold_call(exchange(sums, XY), nz), "z")
    part, sums = grad_call(sums, slopes, passages, local_pos, scale, nxy)

    part = exchange(fold_call(exchange(part, XY), nz), "z")
    part, summed = fold_both_call(part, nxy)
    mine = exchange(part, XY)
    half = dim // 2
    terms = [term_call(notes, mine, first, half) for first in (0, half)]
    others = [lax.ppermute(term, "c", [(0, 1), (1, 0)]) for term in terms]
    grad_projection = join_call(terms, others)

    query_grad = lax.dynamic_slice_in_dim(summed, lax.axis_index("z") * own, own, 0)
    grad_raw = jnp.dot(query_grad, projection.T, precision=lax.Precision.HIGHEST, preferred_element_type=F32)
    first = lax.axis_index(XY) * plane + lax.axis_index("z") * own
    loss = lax.dynamic_slice_in_dim(sums[POS], first, own, 0)
    return (loss, grad_raw, grad_projection)


def solution(mesh):
    axes = Mesh(mesh.devices.reshape(4, 8, 4, 2), ALL)
    in_specs = (P(ALL, None), P(), P(("x", "z", "y"), None), P(ALL, None))
    out_specs = (P(ALL), P(ALL, None), P())
    return jax.shard_map(shards, mesh=axes, in_specs=in_specs, out_specs=out_specs, check_vma=False)
```
